32 devices in a mesh: row: 8 (over y, x, core), col: 4 (over z).
Axes of the slice: x: 2, y: 2, z: 4, core: 2. Of those that a mesh axis runs over, the one named last changes fastest.
Arguments:
- displacement: bfloat16 [65536, 128], P(('row', 'col')), may hold values from -6 to 6
- connectivity: int32 [65536, 8], P(('row', 'col')), may hold values from 0 to 2303, as said below
- element_basis: bfloat16 [4, 32, 32], replicated, may hold values from -1 to 1
- material: float32 [8, 65536], P(None, ('row', 'col')), may hold values from -0.35 to 0.35
- traction: bfloat16 [49152, 128], P(('col', 'row')), may hold values from -6 to 6
- green: bfloat16 [2, 512, 196608], P(None, 'row', 'col'), may hold values from -0.013671875 to 0.013671875
- trace_node: int32 [32, 512], P(('row', 'col')), may hold values from 0 to 2047
- trace_weight: float32 [32, 512], P(('row', 'col')), may hold values from -0.4 to 0.4
- trace_count: int32 [32, 32], P(('row', 'col')), may hold values from 1 to 16
- recv_point: int32 [32, 512], P(('row', 'col')), may hold values from 0 to 3
Outputs:
- fe_out: bfloat16 [65536, 128], P(('row', 'col'))
- boundary_out: float32 [128, 128], P(('row', 'col'))
The draws below stay inside these ranges and needn't reach their ends.
Inputs may be any that keep to these rules, and one draw needn't show every extreme that they name: `connectivity`: entries index a partition's extended numbering: below 128 the previous partition's last nodes, 128 + k its own node k, above that the next partition's first nodes; element k of a partition names only entries from k to k + 256; each partition's first element names 0 and its last names the largest value. `trace_count`: at most 16 live slots from one partition to one owner.
All inputs are finite; a program needn't handle non-finite values.
Results may differ from the reference program's by a relative error of at most 0.013.
Values may be sent and summed in bfloat16 or wider, within the bound.
No kernel may reach another device: no remote copies, remote signals or barrier semaphores. Data moves between devices by JAX's collectives and lax.ppermute only.
A program may use at most 64 MiB of HBM per device.

```python
import jax
import jax.numpy as jnp
from jax import lax

NN = 2048
PTS_DEV = 4
COLS = 196608
CASES = 16
MODES = 4
HALO = 128
SLOT = 16
NODES = 65536
ELEMS = 65536
SLAB_PTS = 128
DEVICES = 32


def draw_connectivity(key, part):
    offset_key = jax.random.fold_in(key, 11)
    offsets = jax.random.randint(offset_key, (DEVICES, NN, 8), 0, 2 * HALO + 1)
    own = jnp.arange(NN, dtype=jnp.int32)[None, :, None]
    links = own + offsets
    links = links.at[:, 0, 0].set(0)
    links = links.at[:, NN - 1, 7].set(NN + 2 * HALO - 1)
    return links.reshape(DEVICES * NN, 8).astype(jnp.int32)


def with_ends(drawn, own_key, smallest, largest):
    shape = drawn.shape
    place = [jax.random.randint(jax.random.fold_in(own_key, axis), (), 0, shape[axis]) for axis in range(len(shape))]
    drawn = drawn.at[tuple(place)].set(smallest)
    longest = shape.index(max(shape))
    place[longest] = (place[longest] + 1) % shape[longest]
    return drawn.at[tuple(place)].set(largest)


def spiked(result, stream_key, source, target, blocks, factor):
    owner, partner = [(jnp.arange(result.shape[position]) // (result.shape[position] // blocks)).reshape([-1 if axis == position else 1 for axis in range(result.ndim)]) for position in (source, target)]
    chosen = jax.random.permutation(stream_key, blocks)[partner]
    strong = (owner == chosen) | (owner == (partner + blocks // 2) % blocks)
    return jnp.where(strong, factor * result, result)


def levels(key, dims, split, least, high):
    factor_of = 1.0
    for dim, blocks in split:
        steps = jax.random.uniform(jax.random.fold_in(jax.random.fold_in(key, 6), dim), (blocks,), jnp.float32, least / len(split), high / len(split))
        factor_of = factor_of * jnp.repeat(jnp.exp(steps), dims[dim] // blocks).reshape((-1,) + (1,) * (len(dims) - 1 - dim))
    return factor_of


def scatter_about(rng, extent, scale, limit, shards=(), kind=jnp.bfloat16):
    factor_of = levels(rng, extent, shards, -0.22, 0.18) if shards else 1.0
    entries = jax.random.normal(rng, extent, jnp.float32) * scale * factor_of
    return jnp.minimum(jnp.maximum(entries, -limit), limit).astype(kind)


def noise_with(rng, extent, deviation, bound, split, heavy, kind=jnp.bfloat16):
    values = deviation * jax.random.normal(rng, extent, jnp.float32)
    if split:
        values = values * levels(rng, extent, split, -0.22, 0.18)
    return jnp.clip(spiked(values, jax.random.fold_in(rng, 3), *heavy), -bound, bound).astype(kind)


def setup_inputs(seed: int = 0) -> dict:
    seeds = jax.random.split(jax.random.key(seed), 11)
    displacement = scatter_about(seeds[0], (NODES, 8 * CASES), 1.0, 6.0, ((0, 32),))
    connectivity = draw_connectivity(jax.random.fold_in(seeds[10], 71), 0)
    element_basis = scatter_about(seeds[2], (MODES, 32, 32), 32 ** -0.5, 1.0)
    material = jnp.clip(jax.random.uniform(seeds[3], (2 * MODES, ELEMS), jnp.float32, -0.35, 0.35) * levels(seeds[3], (2 * MODES, ELEMS), ((1, 32),), -0.4, 0.0), -0.35, 0.35)
    traction = scatter_about(seeds[4], (COLS // 4, 8 * CASES), 1.0, 6.0, ((0, 32),))
    green = noise_with(seeds[5], (2, 4 * SLAB_PTS, COLS), (2 * COLS) ** -0.5, 0.013671875, ((1, 8), (2, 4)), (2, 1, 8, 2.0))
    trace_node = with_ends(jax.random.randint(seeds[6], (DEVICES, DEVICES * SLOT), 0, NN), jax.random.fold_in(seeds[6], 1), 0, NN - 1).astype(jnp.int32)
    trace_weight = scatter_about(seeds[7], (DEVICES, DEVICES * SLOT), 0.06, 0.4, ((0, 32),), jnp.float32)
    trace_count = with_ends(jax.random.randint(seeds[8], (DEVICES, DEVICES), 1, SLOT + 1), jax.random.fold_in(seeds[8], 1), 1, SLOT).astype(jnp.int32)
    recv_point = with_ends(jax.random.randint(seeds[9], (DEVICES, DEVICES * SLOT), 0, PTS_DEV), jax.random.fold_in(seeds[9], 1), 0, PTS_DEV - 1).astype(jnp.int32)
    return dict(displacement=displacement, connectivity=connectivity, element_basis=element_basis, material=material, traction=traction, green=green, trace_node=trace_node, trace_weight=trace_weight, trace_count=trace_count, recv_point=recv_point)


def element_forces(values, basis, coeffs):
    count = values.shape[0]
    lanes = values.shape[2]
    half = lanes // 8
    stacked = values.reshape(count, 32, lanes // 4).astype(jnp.float32)
    modes = jnp.einsum("mij,ejl->meil", basis.astype(jnp.float32), stacked)
    real_c = coeffs[0::2][:, :, None, None]
    imag_c = coeffs[1::2][:, :, None, None]
    real_z = modes[..., :half]
    imag_z = modes[..., half:]
    real_y = jnp.sum(real_c * real_z - imag_c * imag_z, axis=0)
    imag_y = jnp.sum(real_c * imag_z + imag_c * real_z, axis=0)
    return jnp.concatenate([real_y, imag_y], axis=2).reshape(count, 8, lanes)


def reference(displacement, connectivity, element_basis, material, traction, green, trace_node, trace_weight, trace_count, recv_point):
    lanes = displacement.shape[1]
    padded = jnp.pad(displacement, ((HALO, HALO), (0, 0)))
    links_all = connectivity.reshape(DEVICES, NN, 8)
    mats = material.reshape(material.shape[0], DEVICES, NN).transpose(1, 0, 2)

    def one_part(index):
        local = lax.dynamic_slice_in_dim(padded, index * NN, NN + 2 * HALO, 0)
        links = lax.dynamic_index_in_dim(links_all, index, 0, keepdims=False)
        coeffs = lax.dynamic_index_in_dim(mats, index, 0, keepdims=False)
        forces = element_forces(local[links], element_basis, coeffs)
        target = links - HALO
        target = jnp.where((target >= 0) & (target < NN), target, NN)
        summed = jax.ops.segment_sum(forces.reshape(-1, lanes), target.reshape(-1), num_segments=NN)
        return summed.astype(jnp.bfloat16)

    fe_out = lax.map(one_part, jnp.arange(DEVICES, dtype=jnp.int32)).reshape(DEVICES * NN, lanes)

    live = lax.broadcasted_iota(jnp.int32, (DEVICES, DEVICES, SLOT), 2) < trace_count[:, :, None]
    scale = jnp.where(live.reshape(DEVICES, DEVICES * SLOT), trace_weight, jnp.zeros_like(trace_weight))
    source = (jnp.arange(DEVICES, dtype=jnp.int32) * NN)[:, None] + trace_node
    picked = displacement[source]
    values = (picked.astype(jnp.float32) * scale[:, :, None]).astype(jnp.bfloat16)
    arrived = values.reshape(DEVICES, DEVICES, SLOT, lanes).transpose(1, 0, 2, 3).reshape(DEVICES, DEVICES * SLOT, lanes)
    onehot = (recv_point[:, :, None] == jnp.arange(PTS_DEV, dtype=jnp.int32)[None, None, :]).astype(jnp.float32)
    trace_sum = jnp.einsum("dkp,dkl->dpl", onehot, arrived.astype(jnp.float32)).reshape(DEVICES * PTS_DEV, lanes)

    columns = traction.reshape(-1, lanes // 4)
    flat = green.reshape(-1, green.shape[2])
    both = jnp.dot(flat, columns, preferred_element_type=jnp.float32).reshape(2, -1, lanes // 4)
    half = lanes // 8
    real_part = both[0, :, :half] - both[1, :, half:]
    imag_part = both[0, :, half:] + both[1, :, :half]
    slab_product = jnp.concatenate([real_part, imag_part], axis=1).reshape(-1, lanes)
    boundary_out = trace_sum - slab_product
    return fe_out, boundary_out
```

```python
import functools

import jax
import jax.numpy as jnp
from jax import lax
from jax.experimental import pallas as pl
from jax.experimental.pallas import tpu as pltpu
from jax.sharding import PartitionSpec as P

PTS = 4
SLOT = 16
HALO = 128
EB = 256
WIN = EB + 2 * HALO
NT = (((1,), (1,)), ((), ()))
F32 = jnp.float32
BF16 = jnp.bfloat16
VMEM = pl.BlockSpec(memory_space=pltpu.VMEM)


def iota(shape, axis):
    return lax.broadcasted_iota(jnp.int32, shape, axis)


def fe_kernel(low, disp, high, links, basis, material, out, xt, wcat, dist, sel, vs, us, fs, acc):
    nodes = disp.shape[0]
    blocks = nodes // EB
    tiles = nodes // 128

    def place(index, rows):
        xt[:, pl.ds(index * 128, 128)] = rows.astype(F32).T.astype(BF16)

    place(0, low[...])
    for i in range(tiles):
        place(i + 1, disp[i * 128 : (i + 1) * 128, :])
    place(tiles + 1, high[...])

    spread = (iota((256, 32), 0) // 8 == iota((256, 32), 1)).astype(BF16)
    same = iota((256, 256), 0) % 8 == iota((256, 256), 1) % 8
    for m in range(4):
        tall = jnp.dot(spread, basis[m], preferred_element_type=F32).astype(BF16)
        wide = lax.dot_general(tall, spread, NT, preferred_element_type=F32)
        wcat[:, m * 256 : (m + 1) * 256] = jnp.where(same, wide, 0.0).astype(BF16)

    gap = iota((WIN, EB), 0) - iota((WIN, EB), 1)
    dist[...] = jnp.where((gap >= 0) & (gap <= 2 * HALO), gap, -1).astype(F32).astype(BF16)
    acc[...] = jnp.zeros_like(acc)

    def block(b, slot):
        at = pl.multiple_of(b * EB, EB)
        offsets = (links[:, pl.ds(at, EB)] - (at + iota((8, EB), 1))).astype(F32).astype(BF16)
        window = xt[:, pl.ds(at, WIN)]
        for n in range(8):
            hit = dist[...] == offsets[n : n + 1, :]
            chosen = jnp.where(hit, jnp.ones((), BF16), jnp.zeros((), BF16))
            sel[slot, :, n * EB : (n + 1) * EB] = chosen
            v = jnp.dot(window, chosen, preferred_element_type=F32)
            for g in range(4):
                part = jnp.concatenate([v[d * 32 + g * 8 : d * 32 + g * 8 + 8, :] for d in range(4)], axis=0)
                vs[slot, g, n * 32 : (n + 1) * 32, :] = part.astype(BF16)
        coeffs = material[:, pl.ds(at, EB)].astype(F32)
        for h in range(2):
            for n in range(8):
                rows = slice(n * 32, (n + 1) * 32)
                re = vs[slot, h, rows, :].astype(F32)
                im = vs[slot, 2 + h, rows, :].astype(F32)
                for m in range(4):
                    cr = coeffs[2 * m : 2 * m + 1, :]
                    ci = coeffs[2 * m + 1 : 2 * m + 2, :]
                    up = slice(m * 256 + n * 32, m * 256 + (n + 1) * 32)
                    us[slot, h, 0, up, :] = (cr * re - ci * im).astype(BF16)
                    us[slot, h, 1, up, :] = (cr * im + ci * re).astype(BF16)
            for p in range(2):
                f = jnp.dot(wcat[...], us[slot, h, p], preferred_element_type=F32)
                g = 2 * p + h
                for n in range(8):
                    fs[slot, g * 32 : (g + 1) * 32, n * EB : (n + 1) * EB] = f[n * 32 : (n + 1) * 32, :].astype(BF16)
        acc[:, pl.ds(at, WIN)] += lax.dot_general(fs[slot], sel[slot], NT, preferred_element_type=F32)

    def finish(i):
        tile = acc[:, pl.ds(HALO + i * 128, 128)]
        rows = [tile[(g * 4 + d) * 8 : (g * 4 + d) * 8 + 8, :] for d in range(4) for g in range(4)]
        out[pl.ds(i * 128, 128), :] = jnp.concatenate(rows, axis=0).T.astype(BF16)

    def step(i, carry):
        block(2 * i, 0)
        block(2 * i + 1, 1)
        return carry

    lax.fori_loop(0, blocks // 2, step, 0)
    for i in range(tiles):
        finish(i)


def fe_call(low, disp, high, links, basis, material):
    nodes = disp.shape[0]
    return pl.pallas_call(
        fe_kernel,
        out_shape=jax.ShapeDtypeStruct((nodes, 128), BF16),
        in_specs=[pl.BlockSpec(memory_space=pltpu.VMEM)] * 6,
        out_specs=pl.BlockSpec(memory_space=pltpu.VMEM),
        scratch_shapes=[
            pltpu.VMEM((128, nodes + 2 * HALO), BF16),
            pltpu.VMEM((256, 1024), BF16),
            pltpu.VMEM((WIN, EB), BF16),
            pltpu.VMEM((2, WIN, 8 * EB), BF16),
            pltpu.VMEM((2, 4, 256, EB), BF16),
            pltpu.VMEM((2, 2, 2, 1024, EB), BF16),
            pltpu.VMEM((2, 128, 8 * EB), BF16),
            pltpu.VMEM((128, nodes + 2 * HALO), F32),
        ],
        compiler_params=pltpu.CompilerParams(vmem_limit_bytes=24 * 2**20),
        cost_estimate=pl.CostEstimate(flops=nodes * 8000000, bytes_accessed=2**21, transcendentals=0),
    )(low, disp, high, links, basis, material)


def prepare_kernel(rows, cols, traction, disp, node, weight, count, recv, *outs):
    masks = rows // 2
    messages, points = outs[:masks], outs[masks : masks + cols]
    tail, head, slots = outs[masks + cols :]
    lines = traction.shape[0]
    row, col = lax.axis_index("row"), lax.axis_index("col")
    tail[...] = disp[disp.shape[0] - HALO :, :]
    head[...] = disp[:HALO, :]

    widen = (iota((128, 512), 1) // 4 == iota((128, 512), 0)).astype(BF16)
    comp = iota((32, 512), 1) % 4
    for i in range(lines // 128):
        flipped = traction[i * 128 : (i + 1) * 128, :].astype(F32).T.astype(BF16)
        wide = jnp.dot(flipped, widen, preferred_element_type=F32)
        line = wide[:32]
        for k in range(1, 4):
            line = jnp.where(comp == k, wide[k * 32 : (k + 1) * 32], line)
        line = line.astype(BF16)
        for message in messages:
            message[:, i * 512 : (i + 1) * 512] = line

    total = node.shape[1]
    devices = count.shape[1]
    copies = (iota((devices, total), 1) // SLOT == iota((devices, total), 0)).astype(BF16)
    counts = jnp.broadcast_to(count[...].astype(F32), (8, devices)).astype(BF16)
    live = jnp.dot(counts, copies, preferred_element_type=F32)
    scale = jnp.where((iota((8, total), 1) % SLOT).astype(F32) < live, weight[...], 0.0)
    upright = jnp.where(iota((8, total), 0) == 0, node[...].astype(F32), scale).T
    for i in range(total // 256):
        chunk = upright[i * 256 : (i + 1) * 256]
        hit = chunk[:, 0:1] == iota((256, disp.shape[0]), 1).astype(F32)
        picked = jnp.dot(jnp.where(hit, 1.0, 0.0).astype(BF16), disp[...], preferred_element_type=F32)
        slots[i * 256 : (i + 1) * 256, :] = (picked * chunk[:, 1:2]).astype(BF16)

    each = cols * SLOT
    for k in range(masks):
        for core in range(2):
            target = (row // 2 ^ k) * 2 + core
            for t in range(each // 32):
                lane = lines * 4 + (core * (each // 32) + t) * 128
                start = pl.multiple_of(target * each + t * 32, 32)
                messages[k][:, lane : lane + 128] = slots[pl.ds(start, 32), :]

    width = rows * SLOT
    source = iota((total, width), 0)
    place = iota((total, width), 1)
    values = jnp.broadcast_to(recv[...].astype(F32), (8, total)).astype(BF16)
    for s in range(cols):
        other = lax.rem(col + s, cols)
        take = source == (place // SLOT * cols + other) * SLOT + place % SLOT
        points[s][...] = jnp.dot(values, take.astype(BF16), preferred_element_type=F32)


def prepare_call(rows, cols, traction, disp, node, weight, count, recv):
    masks = rows // 2
    message = jax.ShapeDtypeStruct((32, traction.shape[0] * 4 + cols * SLOT * 8), BF16)
    point = jax.ShapeDtypeStruct((8, rows * SLOT), F32)
    halo = jax.ShapeDtypeStruct((HALO, 128), BF16)
    return pl.pallas_call(
        functools.partial(prepare_kernel, rows, cols),
        out_shape=[message] * masks + [point] * cols + [halo] * 2,
        in_specs=[VMEM] * 6,
        out_specs=[VMEM] * (masks + cols + 2),
        scratch_shapes=[pltpu.VMEM((node.shape[1], 128), BF16)],
        compiler_params=pltpu.CompilerParams(vmem_limit_bytes=40 * 2**20),
    )(traction, disp, node, weight, count, recv)


def slab_kernel(rows, cols, green, *refs):
    messages, points = refs[:rows], refs[rows : rows + cols]
    outs = refs[rows + cols : rows + 2 * cols]
    held, sent, traced, total, sems = refs[rows + 2 * cols :]
    row, col = lax.axis_index("row"), lax.axis_index("col")
    high = green.shape[1]
    length = green.shape[2] // rows
    copies = []
    for k in range(rows):
        start = pl.multiple_of((row ^ k) * length, 128)
        copy = pltpu.make_async_copy(green.at[:, :, pl.ds(start, length)], held.at[k], sems.at[k])
        copy.start()
        copies.append(copy)

    each = cols * SLOT
    core = row % 2
    for k in range(rows):
        into = pl.multiple_of((row ^ k) * SLOT, SLOT)
        for t in range(each // 32):
            lane = pl.multiple_of(length + (core * (each // 32) + t) * 128, 128)
            pair = messages[k][:, pl.ds(lane, 128)]
            sent[2 * t, pl.ds(into, SLOT), :] = pair[:SLOT]
            sent[2 * t + 1, pl.ds(into, SLOT), :] = pair[SLOT:]

    both = jnp.zeros((2 * high, 32), F32)
    for k in range(rows):
        copies[k].wait()
        flat = held[k].reshape(2 * high, length)
        both = both + lax.dot_general(flat, messages[k][:, :length], NT, preferred_element_type=F32)
    real = both[:high, :16] - both[high:, 16:]
    imag = both[:high, 16:] + both[high:, :16]
    total[...] = jnp.concatenate([real, imag, jnp.zeros((high, 96), F32)], axis=1)
    for s in range(cols):
        other = lax.rem(col + cols - s, cols)
        hot = (points[s][...] == iota(points[s].shape, 0).astype(F32)).astype(BF16)
        traced[other] = jnp.dot(hot, sent[other], preferred_element_type=F32)
    for c in range(cols):
        parts = [total[pl.ds(c * PTS * 4 + k, PTS, stride=4), :][:, :32] for k in range(4)]
        traced[c, :PTS, :] = traced[c, :PTS, :] - jnp.concatenate(parts, axis=1)
    for s in range(cols):
        outs[s][...] = traced[lax.rem(col + s, cols), :PTS, :]


def slab_call(rows, cols, green, messages, points):
    high = green.shape[1]
    length = green.shape[2] // rows
    part = jax.ShapeDtypeStruct((PTS, 128), F32)
    return pl.pallas_call(
        functools.partial(slab_kernel, rows, cols),
        out_shape=[part] * cols,
        in_specs=[pl.BlockSpec(memory_space=pl.ANY)] + [VMEM] * (rows + cols),
        out_specs=[VMEM] * cols,
        scratch_shapes=[
            pltpu.VMEM((rows, 2, high, length), BF16),
            pltpu.VMEM((cols, rows * SLOT, 128), BF16),
            pltpu.VMEM((cols, 8, 128), F32),
            pltpu.VMEM((high, 128), F32),
            pltpu.SemaphoreType.DMA((rows,)),
        ],
        compiler_params=pltpu.CompilerParams(vmem_limit_bytes=40 * 2**20),
    )(green, *messages, *points)


def shards(rows, cols, displacement, connectivity, element_basis, material, traction, green, node, weight, count, recv):
    made = prepare_call(rows, cols, traction, displacement, node, weight, count, recv)
    masks = rows // 2
    messages, points, (tail, head) = made[:masks], made[masks : masks + cols], made[masks + cols :]
    flat = ("row", "col")
    last = rows * cols - 1
    low = lax.ppermute(tail, flat, [(i, i + 1) for i in range(last)])
    high = lax.ppermute(head, flat, [(i + 1, i) for i in range(last)])

    def across(value, mask):
        return lax.ppermute(value, "row", [(i, i ^ mask) for i in range(rows)])

    def along(value, s):
        return lax.ppermute(value, "col", [(i, (i + s) % cols) for i in range(cols)])

    arrived = [messages[0]] + [across(messages[k], 2 * k) for k in range(1, masks)]
    pairs = [across(value, 1) for value in arrived]
    ordered = [value for both in zip(arrived, pairs) for value in both]
    points = [points[0]] + [along(points[s], s) for s in range(1, cols)]
    fe_out = fe_call(low, displacement, high, connectivity.T, element_basis, material)
    parts = slab_call(rows, cols, green, ordered, points)
    boundary = parts[0]
    for s in range(1, cols):
        boundary = boundary + along(parts[s], s)
    return fe_out, boundary


def solution(mesh):
    rows, cols = mesh.shape["row"], mesh.shape["col"]
    near = P(("row", "col"), None)
    placed = (near, near, P(), P(None, ("row", "col")), P(("col", "row"), None), P(None, "row", "col"), near, near, near, near)
    return jax.shard_map(
        functools.partial(shards, rows, cols),
        mesh=mesh,
        in_specs=placed,
        out_specs=(near, near),
        check_vma=False,
    )
```

```python
import functools

import jax
import jax.numpy as jnp
from jax import lax
from jax.experimental import pallas as pl
from jax.experimental.pallas import tpu as pltpu
from jax.sharding import PartitionSpec as P

PTS = 4
COST = 10**8
SLOT = 16
HALO = 128
EB = 256
WIN = EB + 2 * HALO
NT = (((1,), (1,)), ((), ()))
F32 = jnp.float32
BF16 = jnp.bfloat16
VMEM = pl.BlockSpec(memory_space=pltpu.VMEM)
HBM = pl.BlockSpec(memory_space=pltpu.HBM)


def iota(shape, axis):
    return lax.broadcasted_iota(jnp.int32, shape, axis)


def spread_basis(basis, wcat):
    spread = (iota((256, 32), 0) // 8 == iota((256, 32), 1)).astype(BF16)
    same = iota((256, 256), 0) % 8 == iota((256, 256), 1) % 8
    for m in range(4):
        tall = jnp.dot(spread, basis[m], preferred_element_type=F32).astype(BF16)
        wide = lax.dot_general(tall, spread, NT, preferred_element_type=F32)
        wcat[:, m * 256 : (m + 1) * 256] = jnp.where(same, wide, 0.0).astype(BF16)


def node_gaps():
    gap = iota((WIN, EB), 0) - iota((WIN, EB), 1)
    return jnp.where((gap >= 0) & (gap <= 2 * HALO), gap, -1).astype(F32).astype(BF16)


def flip(rows):
    return rows.astype(F32).T.astype(BF16)


def upright(tile):
    rows = [tile[(g * 4 + d) * 8 : (g * 4 + d) * 8 + 8, :] for d in range(4) for g in range(4)]
    return jnp.concatenate(rows, axis=0).T.astype(BF16)


def element_block(at, window, links, material, wcat, dist, sel, vs, us, fs):
    offsets = (links[:, pl.ds(at, EB)] - (at + iota((8, EB), 1))).astype(F32).astype(BF16)
    for n in range(8):
        hit = dist[...] == offsets[n : n + 1, :]
        chosen = jnp.where(hit, jnp.ones((), BF16), jnp.zeros((), BF16))
        sel[:, n * EB : (n + 1) * EB] = chosen
        v = jnp.dot(window, chosen, preferred_element_type=F32)
        for g in range(4):
            part = jnp.concatenate([v[d * 32 + g * 8 : d * 32 + g * 8 + 8, :] for d in range(4)], axis=0)
            vs[g, n * 32 : (n + 1) * 32, :] = part.astype(BF16)
    coeffs = material[:, pl.ds(at, EB)]
    for h in range(2):
        for n in range(8):
            rows = slice(n * 32, (n + 1) * 32)
            re = vs[h, rows, :].astype(F32)
            im = vs[2 + h, rows, :].astype(F32)
            for m in range(4):
                cr = coeffs[2 * m : 2 * m + 1, :]
                ci = coeffs[2 * m + 1 : 2 * m + 2, :]
                up = slice(m * 256 + n * 32, m * 256 + (n + 1) * 32)
                us[h, 0, up, :] = (cr * re - ci * im).astype(BF16)
                us[h, 1, up, :] = (cr * im + ci * re).astype(BF16)
        for p in range(2):
            f = jnp.dot(wcat[...], us[h, p], preferred_element_type=F32)
            g = 2 * p + h
            for n in range(8):
                fs[g * 32 : (g + 1) * 32, n * EB : (n + 1) * EB] = f[n * 32 : (n + 1) * 32, :].astype(BF16)
    return lax.dot_general(fs[...], sel[...], NT, preferred_element_type=F32)


def inner_kernel(disp, links, basis, material, green, acc, wcat, dist, held, out, xt, sel, vs, us, fs, sems):
    nodes = disp.shape[0]
    pieces = held.shape[0]
    row = lax.axis_index("row")
    copies = []
    for k in range(pieces):
        start = pl.multiple_of((row ^ k) * held.shape[3], 128)
        copy = pltpu.make_async_copy(green.at[:, :, pl.ds(start, held.shape[3])], held.at[k], sems.at[k])
        copy.start()
        copies.append(copy)
    for i in range(nodes // 128):
        xt[:, HALO + i * 128 : HALO + (i + 1) * 128] = flip(disp[i * 128 : (i + 1) * 128, :])
    spread_basis(basis, wcat)
    dist[...] = node_gaps()
    acc[...] = jnp.zeros_like(acc)

    def block(b, k):
        at = pl.multiple_of(b * EB, EB)
        acc[:, pl.ds(at, WIN)] += element_block(
            at, xt[:, pl.ds(at, WIN)], links, material, wcat, dist, sel.at[k], vs.at[k], us.at[k], fs.at[k]
        )

    def step(i, carry):
        block(2 * i + 1, 0)
        block(2 * i + 2, 1)
        return carry

    lax.fori_loop(0, (nodes // EB - 2) // 2, step, 0)
    for i in range((WIN - HALO) // 128, (nodes - WIN + HALO) // 128):
        out[i * 128 : (i + 1) * 128, :] = upright(acc[:, HALO + i * 128 : HALO + (i + 1) * 128])
    for copy in copies:
        copy.wait()


def outer_kernel(before, near, disp, edge, links, material, acc, wcat, dist, out, sel, vs, us, fs, done, sems):
    nodes = disp.shape[0]
    keep = WIN - HALO
    even = lax.axis_index("col") % 2 == 0
    low = jnp.where(even, edge[...], near[:HALO, :])
    high = jnp.where(even, near[:HALO, :], edge[...])
    copies = []
    for e in range(2):
        first = (nodes - keep) * e
        rows = [disp[first + i * 128 : first + (i + 1) * 128, :] for i in range(keep // 128)]
        rows = rows + [high] if e else [low] + rows
        window = jnp.concatenate([flip(tile) for tile in rows], axis=1)
        at = (nodes - EB) * e
        total = acc[:, at : at + WIN] + element_block(
            at, window, links, material, wcat, dist, sel.at[e], vs.at[e], us.at[e], fs.at[e]
        )
        for i in range(keep // 128):
            start = i * 128 if e else HALO + i * 128
            done[e, i * 128 : (i + 1) * 128, :] = upright(total[:, start : start + 128])
        copy = pltpu.make_async_copy(done.at[e], out.at[pl.ds(first, keep), :], sems.at[e])
        copy.start()
        copies.append(copy)
    for copy in copies:
        copy.wait()


def block_scratch():
    return [
        pltpu.VMEM((2, WIN, 8 * EB), BF16),
        pltpu.VMEM((2, 4, 256, EB), BF16),
        pltpu.VMEM((2, 2, 2, 1024, EB), BF16),
        pltpu.VMEM((2, 128, 8 * EB), BF16),
    ]


def element_params(blocks):
    return dict(
        compiler_params=pltpu.CompilerParams(vmem_limit_bytes=16 * 2**20),
        cost_estimate=pl.CostEstimate(flops=blocks * COST, bytes_accessed=2**20, transcendentals=0),
    )


def inner_call(rows, disp, links, basis, material, green):
    nodes = disp.shape[0]
    return pl.pallas_call(
        inner_kernel,
        out_shape=[
            jax.ShapeDtypeStruct((128, nodes + 2 * HALO), F32),
            jax.ShapeDtypeStruct((256, 1024), BF16),
            jax.ShapeDtypeStruct((WIN, EB), BF16),
            jax.ShapeDtypeStruct((rows, 2, green.shape[1], green.shape[2] // rows), BF16),
            jax.ShapeDtypeStruct((nodes, 128), BF16),
        ],
        in_specs=[VMEM] * 4 + [HBM],
        out_specs=[VMEM] * 5,
        scratch_shapes=[pltpu.VMEM((128, nodes + 2 * HALO), BF16)]
        + block_scratch()
        + [pltpu.SemaphoreType.DMA((rows,))],
        **element_params(nodes // EB - 2),
    )(disp, links, basis, material, green)


def outer_call(before, near, disp, edge, links, material, acc, wcat, dist):
    return pl.pallas_call(
        outer_kernel,
        out_shape=jax.ShapeDtypeStruct(before.shape, BF16),
        in_specs=[HBM] + [VMEM] * 8,
        out_specs=HBM,
        scratch_shapes=block_scratch()
        + [pltpu.VMEM((2, WIN - HALO, 128), BF16), pltpu.SemaphoreType.DMA((2,))],
        input_output_aliases={0: 0},
        **element_params(2),
    )(before, near, disp, edge, links, material, acc, wcat, dist)


def prepare_kernel(rows, cols, *refs):
    masks = rows // 2
    sources = refs[:9]
    messages = refs[9 : 9 + masks]
    near, edge, points, disp, links, basis, material, slots, traction, node, weight, count, recv, sems = refs[9 + masks :]
    lines = traction.shape[0]
    row, col = lax.axis_index("row"), lax.axis_index("col")
    pieces = 3 if lines // 128 % 3 == 0 else 1
    share = lines // pieces
    copies = [
        pltpu.make_async_copy(
            sources[0].at[pl.ds(i * share, share), :], traction.at[pl.ds(i * share, share), :], sems.at[8 + i]
        )
        for i in range(pieces)
    ]
    others = [
        pltpu.make_async_copy(sources[i + 1], target, sems.at[i])
        for i, target in enumerate((disp, node, weight, count, recv, links, basis, material))
    ]
    for copy in copies + others:
        copy.start()

    widen = (iota((128, 512), 1) // 4 == iota((128, 512), 0)).astype(BF16)
    comp = iota((32, 512), 1) % 4
    for i in range(lines // 128):
        if i * 128 % share == 0:
            copies[i * 128 // share].wait()
        wide = jnp.dot(flip(traction[i * 128 : (i + 1) * 128, :]), widen, preferred_element_type=F32)
        line = wide[:32]
        for k in range(1, 4):
            line = jnp.where(comp == k, wide[k * 32 : (k + 1) * 32], line)
        line = line.astype(BF16)
        for message in messages:
            message[:, i * 512 : (i + 1) * 512] = line

    for copy in others:
        copy.wait()
    tail, head = disp[disp.shape[0] - HALO :, :], disp[:HALO, :]
    even = col % 2 == 0
    near[:HALO, :] = jnp.where(even, tail, head)
    edge[...] = jnp.where(even, head, tail)
    total = node.shape[1]
    devices = count.shape[1]
    copies = (iota((devices, total), 1) // SLOT == iota((devices, total), 0)).astype(BF16)
    counts = jnp.broadcast_to(count[...].astype(F32), (8, devices)).astype(BF16)
    live = jnp.dot(counts, copies, preferred_element_type=F32)
    scale = jnp.where((iota((8, total), 1) % SLOT).astype(F32) < live, weight[...], 0.0)
    columns = jnp.where(iota((8, total), 0) == 0, node[...].astype(F32), scale).T
    for i in range(total // 256):
        chunk = columns[i * 256 : (i + 1) * 256]
        hit = chunk[:, 0:1] == iota((256, disp.shape[0]), 1).astype(F32)
        picked = jnp.dot(jnp.where(hit, 1.0, 0.0).astype(BF16), disp[...], preferred_element_type=F32)
        slots[i * 256 : (i + 1) * 256, :] = (picked * chunk[:, 1:2]).astype(BF16)

    each = cols * SLOT
    for k in range(masks):
        message, lane = messages[k], lines * 4
        for core in range(2):
            target = (row // 2 ^ k) * 2 + core
            for t in range(each // 32):
                start = pl.multiple_of(target * each + t * 32, 32)
                message[:, lane : lane + 128] = slots[pl.ds(start, 32), :]
                lane += 128

    for t in range(total // 128):
        feeds = recv[:, t * 128 : (t + 1) * 128].astype(F32)
        feeds = jnp.broadcast_to(feeds, (16, 128)).astype(BF16)
        points[t * 16 : (t + 1) * 16, :] = feeds
        near[HALO + t * 16 : HALO + (t + 1) * 16, :] = feeds


def prepare_call(rows, cols, traction, disp, node, weight, count, recv, links, basis, material):
    masks = rows // 2
    message = jax.ShapeDtypeStruct((32, traction.shape[0] * 4 + cols * SLOT * 8), BF16)
    near = jax.ShapeDtypeStruct((HALO + node.shape[1] // 8, 128), BF16)
    edge = jax.ShapeDtypeStruct((HALO, 128), BF16)
    points = jax.ShapeDtypeStruct((node.shape[1] // 8, 128), BF16)
    same = [jax.ShapeDtypeStruct(value.shape, value.dtype) for value in (disp, links, basis, material)]
    return pl.pallas_call(
        functools.partial(prepare_kernel, rows, cols),
        out_shape=[message] * masks + [near, edge, points] + same,
        in_specs=[HBM] * 9,
        out_specs=[VMEM] * (masks + 7),
        scratch_shapes=[pltpu.VMEM((node.shape[1], 128), BF16)]
        + [pltpu.VMEM(value.shape, value.dtype) for value in (traction, node, weight, count, recv)]
        + [pltpu.SemaphoreType.DMA((11,))],
        compiler_params=pltpu.CompilerParams(vmem_limit_bytes=24 * 2**20),
    )(traction, disp, node, weight, count, recv, links, basis, material)


def slab_sum(high, pieces, green, messages, start):
    both = start
    length = green.shape[3]
    for k, message in zip(pieces, messages):
        flat = green[k].reshape(2 * high, length)
        both = both + lax.dot_general(flat, message[:, :length], NT, preferred_element_type=F32)
    return both


def early_kernel(pieces, green, *refs):
    high = green.shape[2]
    refs[-1][...] = slab_sum(high, pieces, green, refs[:-1], jnp.zeros((2 * high, 32), F32))


def early_call(pieces, green, messages):
    return pl.pallas_call(
        functools.partial(early_kernel, pieces),
        out_shape=jax.ShapeDtypeStruct((2 * green.shape[2], 32), F32),
        in_specs=[VMEM] * (1 + len(messages)),
        out_specs=VMEM,
        compiler_params=pltpu.CompilerParams(vmem_limit_bytes=8 * 2**20),
        cost_estimate=pl.CostEstimate(flops=COST, bytes_accessed=2**20, transcendentals=0),
    )(green, *messages)


def late_kernel(rows, cols, pieces, green, before, *refs):
    messages, points = refs[:rows], refs[rows : -cols - 3]
    outs = refs[-cols - 3 : -3]
    sent, traced, total = refs[-3:]
    row, col = lax.axis_index("row"), lax.axis_index("col")
    high = green.shape[2]
    each = cols * SLOT
    for k in range(rows):
        into = pl.multiple_of((row ^ k) * SLOT, SLOT)
        for t in range(each // 32):
            at = pl.multiple_of(green.shape[3] + (row % 2 * (each // 32) + t) * 128, 128)
            pair = messages[k][:, pl.ds(at, 128)]
            sent[2 * t, pl.ds(into, SLOT), :] = pair[:SLOT]
            sent[2 * t + 1, pl.ds(into, SLOT), :] = pair[SLOT:]
    width = rows * SLOT
    length = width * cols
    source, place = iota((length, width), 0), iota((length, width), 1)
    take = (source == (place // SLOT * cols + col) * SLOT + place % SLOT).astype(BF16)
    tall = length // 8
    owners = [block[i * tall : (i + 1) * tall, :] for block in points for i in range(block.shape[0] // tall)]
    for s in range(cols):
        values = jnp.concatenate([owners[s][t * 16 : (t + 1) * 16, :] for t in range(length // 128)], axis=1)
        mine = jnp.dot(values, take, preferred_element_type=F32)[:8]
        hot = (mine == iota(mine.shape, 0).astype(F32)).astype(BF16)
        traced[col ^ s] = jnp.dot(hot, sent[col ^ s], preferred_element_type=F32)

    both = slab_sum(high, pieces, green, [messages[k] for k in pieces], before[...])
    real = both[:high, :16] - both[high:, 16:]
    imag = both[:high, 16:] + both[high:, :16]
    total[...] = jnp.concatenate([real, imag, jnp.zeros((high, 96), F32)], axis=1)
    for c in range(cols):
        parts = [total[pl.ds(c * PTS * 4 + k, PTS, stride=4), :][:, :32] for k in range(4)]
        traced[c, :PTS, :] = traced[c, :PTS, :] - jnp.concatenate(parts, axis=1)
    for s in range(cols):
        outs[s][...] = traced[col ^ s, :PTS, :]


def late_call(rows, cols, pieces, green, before, messages, points):
    return pl.pallas_call(
        functools.partial(late_kernel, rows, cols, pieces),
        out_shape=[jax.ShapeDtypeStruct((PTS, 128), F32)] * cols,
        in_specs=[VMEM] * (2 + rows + len(points)),
        out_specs=[VMEM] * cols,
        scratch_shapes=[
            pltpu.VMEM((cols, rows * SLOT, 128), BF16),
            pltpu.VMEM((cols, 8, 128), F32),
            pltpu.VMEM((green.shape[2], 128), F32),
        ],
        compiler_params=pltpu.CompilerParams(vmem_limit_bytes=8 * 2**20),
        cost_estimate=pl.CostEstimate(flops=COST, bytes_accessed=2**20, transcendentals=0),
    )(green, before, *messages, *points)


def shards(rows, cols, displacement, connectivity, element_basis, material, traction, green, node, weight, count, recv):
    masks = rows // 2
    given = (traction, displacement, node, weight, count, recv, connectivity.T, element_basis, material, green)
    *given, green = [pltpu.with_memory_space_constraint(value, pltpu.HBM) for value in given]
    made = prepare_call(rows, cols, *given)
    messages, (near, edge, points, disp, links, basis, coeffs) = made[:masks], made[masks:]
    flat = ("row", "col")
    last = rows * cols - 1

    def across(value, mask):
        return lax.ppermute(value, "row", [(i, i ^ mask) for i in range(rows)])

    def along(value, s):
        return lax.ppermute(value, "col", [(i, i ^ s) for i in range(cols)])

    chips = [across(messages[k], 2 * k) for k in range(1, masks)]
    near = along(near, 1)
    steps = [(i, i + 1) for i in range(1, last, 2)]
    edge = lax.ppermute(edge, flat, steps + [(b, a) for a, b in steps])
    inner = inner_call(rows, disp, links, basis, coeffs, green)
    own, near, edge, points, inner = lax.optimization_barrier((messages[0], near, edge, points, inner))
    acc, wcat, dist, held, before = inner
    known = [jnp.concatenate([points, near[HALO:]], axis=0)]
    while len(known) < cols // 2:
        known += [along(value, 2 * len(known)) for value in known]
    fe_out = outer_call(before, near, disp, edge, links, coeffs, acc, wcat, dist)
    chips, fe_out, known = lax.optimization_barrier((chips, fe_out, known))
    pair = across(own, 1)
    early = early_call((0,), held, (own,))
    ordered = [own, pair]
    for value in chips:
        ordered += [value, across(value, 1)]
    parts = late_call(rows, cols, tuple(range(1, rows)), held, early, ordered, known)
    boundary = parts[0]
    for value in [along(parts[s], s) for s in range(1, cols)]:
        boundary = boundary + value
    return fe_out, boundary


def solution(mesh):
    rows, cols = mesh.shape["row"], mesh.shape["col"]
    near = P(("row", "col"), None)
    placed = (near, near, P(), P(None, ("row", "col")), P(("col", "row"), None), P(None, "row", "col"), near, near, near, near)
    return jax.shard_map(
        functools.partial(shards, rows, cols),
        mesh=mesh,
        in_specs=placed,
        out_specs=(near, near),
        check_vma=False,
    )
```

```python
import functools

import jax
import jax.numpy as jnp
from jax import lax
from jax.experimental import pallas as pl
from jax.experimental.pallas import tpu as pltpu
from jax.sharding import PartitionSpec as P

PTS = 4
COST = 10**8
SLOT = 16
SPLIT = 5
HALO = 128
EB = 256
WIN = EB + 2 * HALO
NT = (((1,), (1,)), ((), ()))
F32 = jnp.float32
BF16 = jnp.bfloat16
VMEM = pl.BlockSpec(memory_space=pltpu.VMEM)
HBM = pl.BlockSpec(memory_space=pltpu.HBM)


def iota(shape, axis):
    return lax.broadcasted_iota(jnp.int32, shape, axis)


def lane_order():
    row, lane = iota((128, 128), 0), iota((128, 128), 1)
    return (lane == row % 8 // 2 * 32 + row // 8 * 2 + row % 2).astype(F32).astype(BF16)


def spread_basis(basis, wcat):
    spread = (iota((64, 32), 0) // 2 == iota((64, 32), 1)).astype(F32).astype(BF16)
    same = iota((64, 64), 0) % 2 == iota((64, 64), 1) % 2
    wide = []
    for m in range(4):
        tall = jnp.dot(spread, basis[m], preferred_element_type=F32).astype(BF16)
        full = lax.dot_general(tall, spread, NT, preferred_element_type=F32)
        wide.append(jnp.where(same, full, 0.0).astype(BF16))
    wcat[...] = jnp.concatenate(wide, axis=1)


def node_gaps():
    gap = iota((WIN, EB), 0) - iota((WIN, EB), 1)
    return jnp.where((gap >= 0) & (gap <= 2 * HALO), gap, -1).astype(F32).astype(BF16)


def flip(rows, order):
    return lax.dot_general(order, rows, NT, preferred_element_type=F32).astype(BF16)


def upright(tile, order):
    return jnp.dot(tile.T.astype(BF16), order, preferred_element_type=F32).astype(BF16)


def element_gaps():
    gap = iota((EB, WIN), 1) - iota((EB, WIN), 0)
    return jnp.where((gap >= 0) & (gap <= 2 * HALO), gap, -1).astype(F32).astype(BF16)


def gather_steps(at, window, links, dist, dist_t, selt, vs):
    across = links[:, at : at + EB] - (at + iota((8, EB), 1))
    down = across.astype(F32).T.astype(BF16)
    across = across.astype(F32).astype(BF16)
    one, zero = jnp.ones((), BF16), jnp.zeros((), BF16)

    def step(n):
        chosen = jnp.where(dist[...] == across[n : n + 1, :], one, zero)
        vs[n] = jnp.dot(window(), chosen, preferred_element_type=F32)
        selt[n * EB : (n + 1) * EB, :] = jnp.where(dist_t[...] == down[:, n : n + 1], one, zero)

    return [functools.partial(step, n) for n in range(8)]


def force_steps(at, material, wcat, vs, us, fs):
    coeffs = material[:, at : at + EB]
    kept = {}

    def step(cp):
        for n in range(0, 8, 2):
            re = jnp.concatenate([vs[n + i, cp * 8 : cp * 8 + 8, :] for i in range(2)], axis=0)
            im = jnp.concatenate([vs[n + i, 64 + cp * 8 : 72 + cp * 8, :] for i in range(2)], axis=0)
            for m in range(4):
                cr = coeffs[2 * m : 2 * m + 1, :]
                ci = coeffs[2 * m + 1 : 2 * m + 2, :]
                up = slice(m * 64 + n * 8, m * 64 + n * 8 + 16)
                us[cp, up, :EB] = (cr * re - ci * im).astype(BF16)
                us[cp, up, EB:] = (cr * im + ci * re).astype(BF16)
        kept[cp % 2] = jnp.dot(wcat[...], us[cp], preferred_element_type=F32)
        if cp % 2:
            for p in range(2):
                for n in range(8):
                    both = [kept[i][n * 8 : n * 8 + 8, p * EB : (p + 1) * EB] for i in range(2)]
                    rows = slice(p * 64 + cp * 8 - 8, p * 64 + cp * 8 + 8)
                    fs[rows, n * EB : (n + 1) * EB] = jnp.concatenate(both, axis=0).astype(BF16)

    return [functools.partial(step, cp) for cp in range(8)]


def scatter_steps(at, selt, fs, acc):
    def step(i):
        span = slice(i * 2 * EB, (i + 1) * 2 * EB)
        acc[:, at : at + WIN] += jnp.dot(fs[:, span], selt[span, :], preferred_element_type=F32)

    return [functools.partial(step, i) for i in range(4)]


def run_blocks(starts, windows, links, material, wcat, dist, dist_t, selt, vs, us, fs, accs):
    count = len(starts)
    for t in range(count + 2):
        lanes = []
        if t < count:
            lanes.append(gather_steps(starts[t], windows[t], links, dist, dist_t, selt.at[t % 3], vs.at[t % 2]))
        if 0 <= t - 1 < count:
            k = t - 1
            lanes.append(force_steps(starts[k], material, wcat, vs.at[k % 2], us.at[k % 2], fs.at[k % 2]))
        if 0 <= t - 2 < count:
            k = t - 2
            target, at = accs(k)
            lanes.append(scatter_steps(at, selt.at[k % 3], fs.at[k % 2], target))
        for i in range(8):
            for lane in lanes:
                if len(lane) == 8:
                    lane[i]()
                elif i % 2:
                    lane[i // 2]()


def fetch(parity, green, held, sems):
    row = lax.axis_index("row")
    length = held.shape[3]
    copies = []
    for k in range(held.shape[0]):
        start = pl.multiple_of((row ^ (2 * k + parity)) * length, 128)
        copies.append(pltpu.make_async_copy(green.at[:, :, pl.ds(start, length)], held.at[k], sems.at[k]))
    for copy in copies:
        copy.start()
    return copies


def first_kernel(split, disp, links, basis, material, green, acc, xt, wcat, dist, dist_t, held, selt, vs, us, fs, sems):
    nodes = disp.shape[0]
    copies = fetch(0, green, held, sems)
    @pl.when(lax.axis_index("row") >= 0)
    def blocks():
        order = lane_order()
        for i in range(nodes // 256):
            xt[:, HALO + i * 256 : HALO + (i + 1) * 256] = flip(disp[i * 256 : (i + 1) * 256, :], order)
        spread_basis(basis, wcat)
        dist[...] = node_gaps()
        dist_t[...] = element_gaps()
        acc[...] = jnp.zeros_like(acc)
        starts = [b * EB for b in range(1, split)]
        windows = [lambda at=at: xt[:, at : at + WIN] for at in starts]
        run_blocks(starts, windows, links, material, wcat, dist, dist_t, selt, vs, us, fs, lambda k: (acc, starts[k]))

    for copy in copies:
        copy.wait()


def second_kernel(
    split, links, material, before, xt, wcat, dist, dist_t, near, edge, green, acc, out, held, low, selt, vs, us, fs, sems
):
    nodes = links.shape[1]
    copies = fetch(1, green, held, sems)
    @pl.when(lax.axis_index("row") >= 0)
    def blocks():
        order = lane_order()
        even = lax.axis_index("col") % 2 == 0
        low[:, :HALO] = flip(jnp.where(even, edge[...], near[:HALO, :]), order)
        low[:, HALO:] = xt[:, HALO:WIN]
        starts = [b * EB for b in range(split, nodes // EB - 1)] + [0]
        windows = [lambda at=at: xt[:, at : at + WIN] for at in starts[:-1]] + [lambda: low[...]]
        run_blocks(starts, windows, links, material, wcat, dist, dist_t, selt, vs, us, fs, lambda k: (acc, starts[k]))
        for i in range((nodes - WIN + HALO) // 128):
            out[i * 128 : (i + 1) * 128, :] = upright(acc[:, HALO + i * 128 : HALO + (i + 1) * 128], order)

    for copy in copies:
        copy.wait()


def third_kernel(
    before, links, material, acc, xt, wcat, dist, dist_t, near, edge, out, high, last, selt, vs, us, fs, done, sem
):
    nodes = links.shape[1]
    keep = WIN - HALO
    at = nodes - EB
    order = lane_order()
    even = lax.axis_index("col") % 2 == 0
    high[:, :keep] = xt[:, at : at + keep]
    high[:, keep:] = flip(jnp.where(even, near[:HALO, :], edge[...]), order)
    last[...] = acc[:, at : at + WIN]
    windows = [lambda: high[...]]
    run_blocks([at], windows, links, material, wcat, dist, dist_t, selt, vs, us, fs, lambda k: (last, 0))
    for i in range(keep // 128):
        done[i * 128 : (i + 1) * 128, :] = upright(last[:, i * 128 : (i + 1) * 128], order)
    copy = pltpu.make_async_copy(done, out.at[pl.ds(nodes - keep, keep), :], sem)
    copy.start()
    copy.wait()


def block_scratch():
    return [
        pltpu.VMEM((3, 8 * EB, WIN), BF16),
        pltpu.VMEM((2, 8, 128, EB), F32),
        pltpu.VMEM((2, 8, 256, 2 * EB), BF16),
        pltpu.VMEM((2, 128, 8 * EB), BF16),
    ]


def element_params(blocks):
    return dict(
        compiler_params=pltpu.CompilerParams(vmem_limit_bytes=18 * 2**20),
        cost_estimate=pl.CostEstimate(flops=blocks * COST, bytes_accessed=2**20, transcendentals=0),
    )


def held_shape(rows, green):
    return jax.ShapeDtypeStruct((rows // 2, 2, green.shape[1], green.shape[2] // rows), BF16)


def first_call(rows, split, disp, links, basis, material, green):
    wide = disp.shape[0] + 2 * HALO
    return pl.pallas_call(
        functools.partial(first_kernel, split),
        out_shape=[
            jax.ShapeDtypeStruct((128, wide), F32),
            jax.ShapeDtypeStruct((128, wide), BF16),
            jax.ShapeDtypeStruct((64, 256), BF16),
            jax.ShapeDtypeStruct((WIN, EB), BF16),
            jax.ShapeDtypeStruct((EB, WIN), BF16),
            held_shape(rows, green),
        ],
        in_specs=[VMEM] * 4 + [HBM],
        out_specs=[VMEM] * 6,
        scratch_shapes=block_scratch() + [pltpu.SemaphoreType.DMA((rows // 2,))],
        **element_params(split - 1),
    )(disp, links, basis, material, green)


def second_call(rows, split, links, material, acc, shared, near, edge, green):
    nodes = links.shape[1]
    return pl.pallas_call(
        functools.partial(second_kernel, split),
        out_shape=[
            jax.ShapeDtypeStruct(acc.shape, F32),
            jax.ShapeDtypeStruct((nodes, 128), BF16),
            held_shape(rows, green),
        ],
        in_specs=[VMEM] * 9 + [HBM],
        out_specs=[VMEM] * 3,
        scratch_shapes=[pltpu.VMEM((128, WIN), BF16)] + block_scratch() + [pltpu.SemaphoreType.DMA((rows // 2,))],
        input_output_aliases={2: 0},
        **element_params(nodes // EB - split),
    )(links, material, acc, *shared, near, edge, green)


def third_call(before, links, material, acc, shared, near, edge):
    return pl.pallas_call(
        third_kernel,
        out_shape=jax.ShapeDtypeStruct(before.shape, BF16),
        in_specs=[HBM] + [VMEM] * 9,
        out_specs=HBM,
        scratch_shapes=[pltpu.VMEM((128, WIN), BF16), pltpu.VMEM((128, WIN), F32)]
        + block_scratch()
        + [pltpu.VMEM((WIN - HALO, 128), BF16), pltpu.SemaphoreType.DMA],
        input_output_aliases={0: 0},
        **element_params(1),
    )(before, links, material, acc, *shared, near, edge)


def prepare_kernel(rows, cols, *refs):
    masks = rows // 2
    sources = refs[:9]
    messages = refs[9 : 8 + masks]
    near, edge, points, disp, links, basis, material, slots, traction, node, weight, count, recv, sems = refs[8 + masks :]
    lines = traction.shape[0]
    row, col = lax.axis_index("row"), lax.axis_index("col")
    pieces = 3 if lines // 128 % 3 == 0 else 1
    share = lines // pieces
    copies = [
        pltpu.make_async_copy(
            sources[0].at[pl.ds(i * share, share), :], traction.at[pl.ds(i * share, share), :], sems.at[8 + i]
        )
        for i in range(pieces)
    ]
    others = [
        pltpu.make_async_copy(sources[i + 1], target, sems.at[i])
        for i, target in enumerate((disp, node, weight, count, recv, links, basis, material))
    ]
    for copy in copies + others:
        copy.start()

    gap = cols * SLOT * 8
    widen = (iota((128, 512), 1) // 4 == iota((128, 512), 0)).astype(BF16)
    comp = iota((32, 512), 1) % 4
    for i in range(lines // 128):
        if i * 128 % share == 0:
            copies[i * 128 // share].wait()
        wide = jnp.dot(traction[i * 128 : (i + 1) * 128, :].astype(F32).T.astype(BF16), widen, preferred_element_type=F32)
        line = wide[:32]
        for k in range(1, 4):
            line = jnp.where(comp == k, wide[k * 32 : (k + 1) * 32], line)
        line = line.astype(BF16)
        for t in range(2):
            lane = i * 512 + t * 256
            for k, message in enumerate(messages):
                into = lane + gap if k == 1 and lane >= lines * 2 else lane
                message[:, into : into + 256] = line[:, t * 256 : (t + 1) * 256]

    for copy in others:
        copy.wait()
    tail, head = disp[disp.shape[0] - HALO :, :], disp[:HALO, :]
    even = col % 2 == 0
    near[:HALO, :] = jnp.where(even, tail, head)
    edge[...] = jnp.where(even, head, tail)
    total = node.shape[1]
    devices = count.shape[1]
    copies = (iota((devices, total), 1) // SLOT == iota((devices, total), 0)).astype(BF16)
    counts = jnp.broadcast_to(count[...].astype(F32), (8, devices)).astype(BF16)
    live = jnp.dot(counts, copies, preferred_element_type=F32)
    scale = jnp.where((iota((8, total), 1) % SLOT).astype(F32) < live, weight[...], 0.0)
    columns = jnp.where(iota((8, total), 0) == 0, node[...].astype(F32), scale).T
    for i in range(total // 256):
        chunk = columns[i * 256 : (i + 1) * 256]
        hit = chunk[:, 0:1] == iota((256, disp.shape[0]), 1).astype(F32)
        picked = jnp.dot(jnp.where(hit, 1.0, 0.0).astype(BF16), disp[...], preferred_element_type=F32)
        slots[i * 256 : (i + 1) * 256, :] = (picked * chunk[:, 1:2]).astype(BF16)

    each = cols * SLOT
    places = [(messages[k], lines * 4) for k in range(3)] + [(messages[1], lines * 2)]
    places[1] = (messages[1], lines * 4 + gap)
    places += [(message, lines * 4) for message in messages[3:]]
    for k, (message, lane) in enumerate(places):
        for core in range(2):
            target = (row // 2 ^ k) * 2 + core
            for t in range(each // 32):
                start = pl.multiple_of(target * each + t * 32, 32)
                message[:, lane : lane + 128] = slots[pl.ds(start, 32), :]
                lane += 128

    for t in range(total // 128):
        feeds = recv[:, t * 128 : (t + 1) * 128].astype(F32)
        feeds = jnp.broadcast_to(feeds, (16, 128)).astype(BF16)
        points[t * 16 : (t + 1) * 16, :] = feeds
        near[HALO + t * 16 : HALO + (t + 1) * 16, :] = feeds


def prepare_call(rows, cols, traction, disp, node, weight, count, recv, links, basis, material):
    masks = rows // 2
    width = traction.shape[0] * 4 + cols * SLOT * 8
    widths = [width, width + cols * SLOT * 8] + [width] * (masks - 3)
    near = jax.ShapeDtypeStruct((HALO + node.shape[1] // 8, 128), BF16)
    edge = jax.ShapeDtypeStruct((HALO, 128), BF16)
    points = jax.ShapeDtypeStruct((node.shape[1] // 8, 128), BF16)
    same = [jax.ShapeDtypeStruct(value.shape, value.dtype) for value in (disp, links, basis, material)]
    return pl.pallas_call(
        functools.partial(prepare_kernel, rows, cols),
        out_shape=[jax.ShapeDtypeStruct((32, width), BF16) for width in widths] + [near, edge, points] + same,
        in_specs=[HBM] * 9,
        out_specs=[VMEM] * (masks + 6),
        scratch_shapes=[pltpu.VMEM((node.shape[1], 128), BF16)]
        + [pltpu.VMEM(value.shape, value.dtype) for value in (traction, node, weight, count, recv)]
        + [pltpu.SemaphoreType.DMA((11,))],
        compiler_params=pltpu.CompilerParams(vmem_limit_bytes=24 * 2**20),
    )(traction, disp, node, weight, count, recv, links, basis, material)


def slab_sum(high, plan, green, messages, start):
    both = start
    for which, lane, width, k, into in plan:
        flat = green[k // 2, :, :, into : into + width].reshape(2 * high, width)
        both = both + lax.dot_general(flat, messages[which][:, lane : lane + width], NT, preferred_element_type=F32)
    return both


def early_kernel(plan, green, *refs):
    high = green.shape[2]
    refs[-1][...] = slab_sum(high, plan, green, refs[:-1], jnp.zeros((2 * high, 32), F32))


def early_call(plan, green, messages):
    return pl.pallas_call(
        functools.partial(early_kernel, plan),
        out_shape=jax.ShapeDtypeStruct((2 * green.shape[2], 32), F32),
        in_specs=[VMEM] * (1 + len(messages)),
        out_specs=VMEM,
        compiler_params=pltpu.CompilerParams(vmem_limit_bytes=8 * 2**20),
        cost_estimate=pl.CostEstimate(flops=COST, bytes_accessed=2**20, transcendentals=0),
    )(green, *messages)


def late_kernel(rows, cols, plan, slots, green, before, *refs):
    count = 2 * (max(entry[0] for entry in plan) + 1)
    messages, points = refs[:count], refs[count : -cols - 3]
    outs = refs[-cols - 3 : -3]
    sent, traced, total = refs[-3:]
    row, col = lax.axis_index("row"), lax.axis_index("col")
    high = green.shape[2]
    each = cols * SLOT
    for which, lane, k in slots:
        for core in range(2):
            into = pl.multiple_of((row ^ k ^ core) * SLOT, SLOT)
            for t in range(each // 32):
                at = pl.multiple_of(lane + (row % 2 * (each // 32) + t) * 128, 128)
                pair = messages[which + core * (count // 2)][:, pl.ds(at, 128)]
                sent[2 * t, pl.ds(into, SLOT), :] = pair[:SLOT]
                sent[2 * t + 1, pl.ds(into, SLOT), :] = pair[SLOT:]
    width = rows * SLOT
    length = width * cols
    source, place = iota((length, width), 0), iota((length, width), 1)
    take = (source == (place // SLOT * cols + col) * SLOT + place % SLOT).astype(BF16)
    tall = length // 8
    owners = [block[i * tall : (i + 1) * tall, :] for block in points for i in range(block.shape[0] // tall)]
    for s in range(cols):
        values = jnp.concatenate([owners[s][t * 16 : (t + 1) * 16, :] for t in range(length // 128)], axis=1)
        mine = jnp.dot(values, take, preferred_element_type=F32)[:8]
        hot = (mine == iota(mine.shape, 0).astype(F32)).astype(BF16)
        traced[col ^ s] = jnp.dot(hot, sent[col ^ s], preferred_element_type=F32)

    both = slab_sum(high, plan, green, messages[count // 2 :], before[...])
    real = both[:high, :16] - both[high:, 16:]
    imag = both[:high, 16:] + both[high:, :16]
    total[...] = jnp.concatenate([real, imag, jnp.zeros((high, 96), F32)], axis=1)
    for c in range(cols):
        parts = [total[pl.ds(c * PTS * 4 + k, PTS, stride=4), :][:, :32] for k in range(4)]
        traced[c, :PTS, :] = traced[c, :PTS, :] - jnp.concatenate(parts, axis=1)
    for s in range(cols):
        outs[s][...] = traced[col ^ s, :PTS, :]


def late_call(rows, cols, plan, slots, green, before, messages, points):
    return pl.pallas_call(
        functools.partial(late_kernel, rows, cols, plan, slots),
        out_shape=[jax.ShapeDtypeStruct((PTS, 128), F32)] * cols,
        in_specs=[VMEM] * (2 + len(messages) + len(points)),
        out_specs=[VMEM] * cols,
        scratch_shapes=[
            pltpu.VMEM((cols, rows * SLOT, 128), BF16),
            pltpu.VMEM((cols, 8, 128), F32),
            pltpu.VMEM((green.shape[2], 128), F32),
        ],
        compiler_params=pltpu.CompilerParams(vmem_limit_bytes=8 * 2**20),
        cost_estimate=pl.CostEstimate(flops=COST, bytes_accessed=2**20, transcendentals=0),
    )(green, before, *messages, *points)


def shards(rows, cols, displacement, connectivity, element_basis, material, traction, green, node, weight, count, recv):
    masks = rows // 2
    given = (traction, displacement, node, weight, count, recv, connectivity.T, element_basis, material, green)
    *given, green = [pltpu.with_memory_space_constraint(value, pltpu.HBM) for value in given]
    made = prepare_call(rows, cols, *given)
    messages, (near, edge, points, disp, links, basis, coeffs) = made[: masks - 1], made[masks - 1 :]
    flat = ("row", "col")
    last = rows * cols - 1
    half = traction.shape[0] * 2
    each = cols * SLOT * 8

    def across(value, mask):
        return lax.ppermute(value, "row", [(i, i ^ mask) for i in range(rows)])

    def along(value, s):
        return lax.ppermute(value, "col", [(i, i ^ s) for i in range(cols)])

    own = messages[0]
    beside, below = across(messages[1], 2), across(messages[2], 4)
    far = [across(messages[k], 2 * k + 2) for k in range(3, masks - 1)]
    near = along(near, 1)
    steps = [(i, i + 1) for i in range(1, last, 2)]
    edge = lax.ppermute(edge, flat, steps + [(b, a) for a, b in steps])
    made = first_call(rows, SPLIT, disp, links, basis, coeffs, green)
    own, beside, below, near, edge, points, made = lax.optimization_barrier(
        (own, beside, below, near, edge, points, made)
    )
    acc, *shared, held = made
    cross = [across(beside[:, : half + each], 4), across(below[:, half : 2 * half], 2)]
    known = [jnp.concatenate([points, near[HALO:]], axis=0)]
    while len(known) < cols // 2:
        known += [along(value, 2 * len(known)) for value in known]
    acc, before, held_pair = second_call(rows, SPLIT, links, coeffs, acc, shared, near, edge, green)
    own, beside, below, cross, far, known, before, held_pair = lax.optimization_barrier(
        (own, beside, below, cross, far, known, before, held_pair)
    )
    here = [own, beside, below] + cross + far
    there = [across(value, 1) for value in here]
    plan = [(0, 0, 2 * half, 0, 0), (1, 0, half, 2, 0), (1, half + each, half, 2, half), (2, 0, 2 * half, 4, 0)]
    plan += [(3, 0, half, 6, 0), (4, 0, half, 6, half)]
    slots = [(0, 2 * half, 0), (1, 2 * half + each, 2), (2, 2 * half, 4), (3, half, 6)]
    for i in range(len(far)):
        plan.append((5 + i, 0, 2 * half, 8 + 2 * i, 0))
        slots.append((5 + i, 2 * half, 8 + 2 * i))
    early = early_call(plan, held, here)
    early, there = lax.optimization_barrier((early, there))
    plan = [(which, lane, width, k + 1, into) for which, lane, width, k, into in plan]
    parts = late_call(rows, cols, plan, slots, held_pair, early, here + there, known)
    sums = [along(parts[s], s) for s in range(1, cols)]
    before, total = lax.optimization_barrier((before, parts[0]))
    fe_out = third_call(before, links, coeffs, acc, shared, near, edge)
    sums, fe_out = lax.optimization_barrier((sums, fe_out))
    boundary = total
    for value in sums:
        boundary = boundary + value
    return fe_out, boundary


def solution(mesh):
    rows, cols = mesh.shape["row"], mesh.shape["col"]
    near = P(("row", "col"), None)
    placed = (near, near, P(), P(None, ("row", "col")), P(("col", "row"), None), P(None, "row", "col"), near, near, near, near)
    return jax.shard_map(
        functools.partial(shards, rows, cols),
        mesh=mesh,
        in_specs=placed,
        out_specs=(near, near),
        check_vma=False,
    )
```

```python
import functools

import jax
import jax.numpy as jnp
from jax import lax
from jax.experimental import pallas as pl
from jax.experimental.pallas import tpu as pltpu
from jax.sharding import PartitionSpec as P

PTS = 4
COST = 10**8
SLOT = 16
SPLIT = 6
HALO = 128
EB = 256
WIN = EB + 2 * HALO
NT = (((1,), (1,)), ((), ()))
F32 = jnp.float32
BF16 = jnp.bfloat16
VMEM = pl.BlockSpec(memory_space=pltpu.VMEM)
HBM = pl.BlockSpec(memory_space=pltpu.HBM)


def iota(shape, axis):
    return lax.broadcasted_iota(jnp.int32, shape, axis)


def lane_order():
    row, lane = iota((128, 128), 0), iota((128, 128), 1)
    return (lane == row % 8 // 2 * 32 + row // 8 * 2 + row % 2).astype(F32).astype(BF16)


def spread_basis(basis, wcat):
    spread = (iota((64, 32), 0) // 2 == iota((64, 32), 1)).astype(F32).astype(BF16)
    same = iota((64, 64), 0) % 2 == iota((64, 64), 1) % 2
    wide = []
    for m in range(4):
        tall = jnp.dot(spread, basis[m], preferred_element_type=F32).astype(BF16)
        full = lax.dot_general(tall, spread, NT, preferred_element_type=F32)
        wide.append(jnp.where(same, full, 0.0).astype(BF16))
    wcat[...] = jnp.concatenate(wide, axis=1)


def node_gaps():
    gap = iota((WIN, EB), 0) - iota((WIN, EB), 1)
    return jnp.where((gap >= 0) & (gap <= 2 * HALO), gap, -1).astype(F32).astype(BF16)


def flip(rows, order):
    return lax.dot_general(order, rows, NT, preferred_element_type=F32).astype(BF16)


def upright(tile, order):
    return jnp.dot(tile.T.astype(BF16), order, preferred_element_type=F32).astype(BF16)


def element_gaps():
    gap = iota((EB, WIN), 1) - iota((EB, WIN), 0)
    return jnp.where((gap >= 0) & (gap <= 2 * HALO), gap, -1).astype(F32).astype(BF16)


def gather_steps(at, window, links, dist, dist_t, selt, vs):
    across = links[:, at : at + EB] - (at + iota((8, EB), 1))
    down = across.astype(F32).T.astype(BF16)
    across = across.astype(F32).astype(BF16)
    one, zero = jnp.ones((), BF16), jnp.zeros((), BF16)

    def step(n):
        chosen = jnp.where(dist[...] == across[n : n + 1, :], one, zero)
        vs[n] = jnp.dot(window(), chosen, preferred_element_type=F32)
        selt[n * EB : (n + 1) * EB, :] = jnp.where(dist_t[...] == down[:, n : n + 1], one, zero)

    return [functools.partial(step, n) for n in range(8)]


def force_steps(at, material, wcat, vs, us, fs):
    coeffs = material[:, at : at + EB]
    kept = {}

    def step(cp):
        for n in range(0, 8, 2):
            re = jnp.concatenate([vs[n + i, cp * 8 : cp * 8 + 8, :] for i in range(2)], axis=0)
            im = jnp.concatenate([vs[n + i, 64 + cp * 8 : 72 + cp * 8, :] for i in range(2)], axis=0)
            for m in range(4):
                cr = coeffs[2 * m : 2 * m + 1, :]
                ci = coeffs[2 * m + 1 : 2 * m + 2, :]
                up = slice(m * 64 + n * 8, m * 64 + n * 8 + 16)
                us[cp, up, :EB] = (cr * re - ci * im).astype(BF16)
                us[cp, up, EB:] = (cr * im + ci * re).astype(BF16)
        kept[cp % 2] = jnp.dot(wcat[...], us[cp], preferred_element_type=F32)
        if cp % 2:
            for p in range(2):
                for n in range(8):
                    both = [kept[i][n * 8 : n * 8 + 8, p * EB : (p + 1) * EB] for i in range(2)]
                    rows = slice(p * 64 + cp * 8 - 8, p * 64 + cp * 8 + 8)
                    fs[rows, n * EB : (n + 1) * EB] = jnp.concatenate(both, axis=0).astype(BF16)

    return [functools.partial(step, cp) for cp in range(8)]


def scatter_steps(at, selt, fs, acc):
    def step(i):
        span = slice(i * 2 * EB, (i + 1) * 2 * EB)
        acc[:, at : at + WIN] += jnp.dot(fs[:, span], selt[span, :], preferred_element_type=F32)

    return [functools.partial(step, i) for i in range(4)]


def run_blocks(starts, windows, links, material, wcat, dist, dist_t, selt, vs, us, fs, accs):
    count = len(starts)
    for t in range(count + 2):
        lanes = []
        if t < count:
            lanes.append(gather_steps(starts[t], windows[t], links, dist, dist_t, selt.at[t % 3], vs.at[t % 2]))
        if 0 <= t - 1 < count:
            k = t - 1
            lanes.append(force_steps(starts[k], material, wcat, vs.at[k % 2], us.at[k % 2], fs.at[k % 2]))
        if 0 <= t - 2 < count:
            k = t - 2
            target, at = accs(k)
            lanes.append(scatter_steps(at, selt.at[k % 3], fs.at[k % 2], target))
        for i in range(8):
            for lane in lanes:
                if len(lane) == 8:
                    lane[i]()
                elif i % 2:
                    lane[i // 2]()


def fetch(parity, green, held, sems):
    row = lax.axis_index("row")
    length = held.shape[3]
    copies = []
    for k in range(held.shape[0]):
        start = pl.multiple_of((row ^ (2 * k + parity)) * length, 128)
        copies.append(pltpu.make_async_copy(green.at[:, :, pl.ds(start, length)], held.at[k], sems.at[k]))
    for copy in copies:
        copy.start()
    return copies


def first_kernel(split, disp, links, basis, material, green, acc, xt, wcat, dist, dist_t, held, selt, vs, us, fs, sems):
    nodes = disp.shape[0]
    copies = fetch(0, green, held, sems)
    @pl.when(lax.axis_index("row") >= 0)
    def blocks():
        order = lane_order()
        for i in range(nodes // 256):
            xt[:, HALO + i * 256 : HALO + (i + 1) * 256] = flip(disp[i * 256 : (i + 1) * 256, :], order)
        spread_basis(basis, wcat)
        dist[...] = node_gaps()
        dist_t[...] = element_gaps()
        acc[...] = jnp.zeros_like(acc)
        starts = [b * EB for b in range(1, split)]
        windows = [lambda at=at: xt[:, at : at + WIN] for at in starts]
        run_blocks(starts, windows, links, material, wcat, dist, dist_t, selt, vs, us, fs, lambda k: (acc, starts[k]))

    for copy in copies:
        copy.wait()


def second_kernel(
    split, links, material, before, xt, wcat, dist, dist_t, near, edge, green, acc, held, low, selt, vs, us, fs, sems
):
    nodes = links.shape[1]
    copies = fetch(1, green, held, sems)
    @pl.when(lax.axis_index("row") >= 0)
    def blocks():
        order = lane_order()
        even = lax.axis_index("col") % 2 == 0
        low[:, :HALO] = flip(jnp.where(even, edge[...], near[:HALO, :]), order)
        low[:, HALO:] = xt[:, HALO:WIN]
        starts = [b * EB for b in range(split, nodes // EB - 1)] + [0]
        windows = [lambda at=at: xt[:, at : at + WIN] for at in starts[:-1]] + [lambda: low[...]]
        run_blocks(starts, windows, links, material, wcat, dist, dist_t, selt, vs, us, fs, lambda k: (acc, starts[k]))
    for copy in copies:
        copy.wait()


def third_kernel(
    links, material, acc, xt, wcat, dist, dist_t, near, edge, out, high, last, selt, vs, us, fs, done, sems
):
    nodes = links.shape[1]
    keep = WIN - HALO
    at = nodes - EB
    order = lane_order()
    even = lax.axis_index("col") % 2 == 0
    high[:, :keep] = xt[:, at : at + keep]
    high[:, keep:] = flip(jnp.where(even, near[:HALO, :], edge[...]), order)
    last[...] = acc[:, at : at + WIN]
    split = nodes - keep
    for i in range(split // 128):
        done[i * 128 : (i + 1) * 128, :] = upright(acc[:, HALO + i * 128 : HALO + (i + 1) * 128], order)
    copies = [
        pltpu.make_async_copy(done.at[pl.ds(0, split), :], out.at[pl.ds(0, split), :], sems.at[0]),
        pltpu.make_async_copy(done.at[pl.ds(split, keep), :], out.at[pl.ds(split, keep), :], sems.at[1]),
    ]
    copies[0].start()
    windows = [lambda: high[...]]
    run_blocks([at], windows, links, material, wcat, dist, dist_t, selt, vs, us, fs, lambda k: (last, 0))
    for i in range(keep // 128):
        done[split + i * 128 : split + (i + 1) * 128, :] = upright(last[:, i * 128 : (i + 1) * 128], order)
    copies[1].start()
    for copy in copies:
        copy.wait()


def block_scratch():
    return [
        pltpu.VMEM((3, 8 * EB, WIN), BF16),
        pltpu.VMEM((2, 8, 128, EB), F32),
        pltpu.VMEM((2, 8, 256, 2 * EB), BF16),
        pltpu.VMEM((2, 128, 8 * EB), BF16),
    ]


def element_params(blocks):
    return dict(
        compiler_params=pltpu.CompilerParams(vmem_limit_bytes=18 * 2**20),
        cost_estimate=pl.CostEstimate(flops=blocks * COST, bytes_accessed=2**20, transcendentals=0),
    )


def held_shape(rows, green):
    return jax.ShapeDtypeStruct((rows // 2, 2, green.shape[1], green.shape[2] // rows), BF16)


def first_call(rows, split, disp, links, basis, material, green):
    wide = disp.shape[0] + 2 * HALO
    return pl.pallas_call(
        functools.partial(first_kernel, split),
        out_shape=[
            jax.ShapeDtypeStruct((128, wide), F32),
            jax.ShapeDtypeStruct((128, wide), BF16),
            jax.ShapeDtypeStruct((64, 256), BF16),
            jax.ShapeDtypeStruct((WIN, EB), BF16),
            jax.ShapeDtypeStruct((EB, WIN), BF16),
            held_shape(rows, green),
        ],
        in_specs=[VMEM] * 4 + [HBM],
        out_specs=[VMEM] * 6,
        scratch_shapes=block_scratch() + [pltpu.SemaphoreType.DMA((rows // 2,))],
        **element_params(split - 1),
    )(disp, links, basis, material, green)


def second_call(rows, split, links, material, acc, shared, near, edge, green):
    nodes = links.shape[1]
    return pl.pallas_call(
        functools.partial(second_kernel, split),
        out_shape=[
            jax.ShapeDtypeStruct(acc.shape, F32),
            held_shape(rows, green),
        ],
        in_specs=[VMEM] * 9 + [HBM],
        out_specs=[VMEM] * 2,
        scratch_shapes=[pltpu.VMEM((128, WIN), BF16)] + block_scratch() + [pltpu.SemaphoreType.DMA((rows // 2,))],
        input_output_aliases={2: 0},
        **element_params(nodes // EB - split),
    )(links, material, acc, *shared, near, edge, green)


def third_call(links, material, acc, shared, near, edge):
    nodes = links.shape[1]
    return pl.pallas_call(
        third_kernel,
        out_shape=jax.ShapeDtypeStruct((nodes, 128), BF16),
        in_specs=[VMEM] * 9,
        out_specs=HBM,
        scratch_shapes=[pltpu.VMEM((128, WIN), BF16), pltpu.VMEM((128, WIN), F32)]
        + block_scratch()
        + [pltpu.VMEM((nodes, 128), BF16), pltpu.SemaphoreType.DMA((2,))],
        **element_params(1),
    )(links, material, acc, *shared, near, edge)


def prepare_kernel(rows, cols, *refs):
    masks = rows // 2
    sources = refs[:9]
    messages = refs[9 : 8 + masks]
    near, edge, points, disp, links, basis, material, slots, traction, node, weight, count, recv, sems = refs[8 + masks :]
    lines = traction.shape[0]
    row, col = lax.axis_index("row"), lax.axis_index("col")
    pieces = 3 if lines // 128 % 3 == 0 else 1
    share = lines // pieces
    copies = [
        pltpu.make_async_copy(
            sources[0].at[pl.ds(i * share, share), :], traction.at[pl.ds(i * share, share), :], sems.at[8 + i]
        )
        for i in range(pieces)
    ]
    others = [
        pltpu.make_async_copy(sources[i + 1], target, sems.at[i])
        for i, target in enumerate((disp, node, weight, count, recv, links, basis, material))
    ]
    for copy in copies + others:
        copy.start()

    gap = cols * SLOT * 8
    widen = (iota((128, 512), 1) // 4 == iota((128, 512), 0)).astype(BF16)
    comp = iota((32, 512), 1) % 4
    for i in range(lines // 128):
        if i * 128 % share == 0:
            copies[i * 128 // share].wait()
        wide = jnp.dot(traction[i * 128 : (i + 1) * 128, :].astype(F32).T.astype(BF16), widen, preferred_element_type=F32)
        line = wide[:32]
        for k in range(1, 4):
            line = jnp.where(comp == k, wide[k * 32 : (k + 1) * 32], line)
        line = line.astype(BF16)
        for t in range(2):
            lane = i * 512 + t * 256
            for k, message in enumerate(messages):
                into = lane + gap if k == 1 and lane >= lines * 2 else lane
                message[:, into : into + 256] = line[:, t * 256 : (t + 1) * 256]

    for copy in others:
        copy.wait()
    tail, head = disp[disp.shape[0] - HALO :, :], disp[:HALO, :]
    even = col % 2 == 0
    near[:HALO, :] = jnp.where(even, tail, head)
    edge[...] = jnp.where(even, head, tail)
    total = node.shape[1]
    devices = count.shape[1]
    copies = (iota((devices, total), 1) // SLOT == iota((devices, total), 0)).astype(BF16)
    counts = jnp.broadcast_to(count[...].astype(F32), (8, devices)).astype(BF16)
    live = jnp.dot(counts, copies, preferred_element_type=F32)
    scale = jnp.where((iota((8, total), 1) % SLOT).astype(F32) < live, weight[...], 0.0)
    columns = jnp.where(iota((8, total), 0) == 0, node[...].astype(F32), scale).T
    for i in range(total // 256):
        chunk = columns[i * 256 : (i + 1) * 256]
        hit = chunk[:, 0:1] == iota((256, disp.shape[0]), 1).astype(F32)
        picked = jnp.dot(jnp.where(hit, 1.0, 0.0).astype(BF16), disp[...], preferred_element_type=F32)
        slots[i * 256 : (i + 1) * 256, :] = (picked * chunk[:, 1:2]).astype(BF16)

    each = cols * SLOT
    places = [(messages[k], lines * 4) for k in range(3)] + [(messages[1], lines * 2)]
    places[1] = (messages[1], lines * 4 + gap)
    places += [(message, lines * 4) for message in messages[3:]]
    for k, (message, lane) in enumerate(places):
        for core in range(2):
            target = (row // 2 ^ k) * 2 + core
            for t in range(each // 32):
                start = pl.multiple_of(target * each + t * 32, 32)
                message[:, lane : lane + 128] = slots[pl.ds(start, 32), :]
                lane += 128

    for t in range(total // 128):
        feeds = recv[:, t * 128 : (t + 1) * 128].astype(F32)
        feeds = jnp.broadcast_to(feeds, (16, 128)).astype(BF16)
        points[t * 16 : (t + 1) * 16, :] = feeds
        near[HALO + t * 16 : HALO + (t + 1) * 16, :] = feeds


def prepare_call(rows, cols, traction, disp, node, weight, count, recv, links, basis, material):
    masks = rows // 2
    width = traction.shape[0] * 4 + cols * SLOT * 8
    widths = [width, width + cols * SLOT * 8] + [width] * (masks - 3)
    near = jax.ShapeDtypeStruct((HALO + node.shape[1] // 8, 128), BF16)
    edge = jax.ShapeDtypeStruct((HALO, 128), BF16)
    points = jax.ShapeDtypeStruct((node.shape[1] // 8, 128), BF16)
    same = [jax.ShapeDtypeStruct(value.shape, value.dtype) for value in (disp, links, basis, material)]
    return pl.pallas_call(
        functools.partial(prepare_kernel, rows, cols),
        out_shape=[jax.ShapeDtypeStruct((32, width), BF16) for width in widths] + [near, edge, points] + same,
        in_specs=[HBM] * 9,
        out_specs=[VMEM] * (masks + 6),
        scratch_shapes=[pltpu.VMEM((node.shape[1], 128), BF16)]
        + [pltpu.VMEM(value.shape, value.dtype) for value in (traction, node, weight, count, recv)]
        + [pltpu.SemaphoreType.DMA((11,))],
        compiler_params=pltpu.CompilerParams(vmem_limit_bytes=24 * 2**20),
    )(traction, disp, node, weight, count, recv, links, basis, material)


def slab_sum(high, plan, green, messages, start):
    both = start
    for which, lane, width, k, into in plan:
        flat = green[k // 2, :, :, into : into + width].reshape(2 * high, width)
        both = both + lax.dot_general(flat, messages[which][:, lane : lane + width], NT, preferred_element_type=F32)
    return both


def early_kernel(plan, count, green, *refs):
    high = green.shape[2]
    start = refs[count][...] if len(refs) > count + 1 else jnp.zeros((2 * high, 32), F32)
    refs[-1][...] = slab_sum(high, plan, green, refs[:count], start)


def early_call(plan, green, messages, start=()):
    return pl.pallas_call(
        functools.partial(early_kernel, plan, len(messages)),
        out_shape=jax.ShapeDtypeStruct((2 * green.shape[2], 32), F32),
        in_specs=[VMEM] * (1 + len(messages) + len(start)),
        out_specs=VMEM,
        compiler_params=pltpu.CompilerParams(vmem_limit_bytes=8 * 2**20),
        cost_estimate=pl.CostEstimate(flops=COST, bytes_accessed=2**20, transcendentals=0),
    )(green, *messages, *start)


def late_kernel(rows, cols, plan, slots, green, before, *refs):
    count = 2 * (max(entry[0] for entry in plan) + 1)
    messages, points = refs[:count], refs[count : -cols - 3]
    outs = refs[-cols - 3 : -3]
    sent, traced, total = refs[-3:]
    row, col = lax.axis_index("row"), lax.axis_index("col")
    high = green.shape[2]
    each = cols * SLOT
    for which, lane, k in slots:
        for core in range(2):
            into = pl.multiple_of((row ^ k ^ core) * SLOT, SLOT)
            for t in range(each // 32):
                at = pl.multiple_of(lane + (row % 2 * (each // 32) + t) * 128, 128)
                pair = messages[which + core * (count // 2)][:, pl.ds(at, 128)]
                sent[2 * t, pl.ds(into, SLOT), :] = pair[:SLOT]
                sent[2 * t + 1, pl.ds(into, SLOT), :] = pair[SLOT:]
    width = rows * SLOT
    length = width * cols
    source, place = iota((length, width), 0), iota((length, width), 1)
    take = (source == (place // SLOT * cols + col) * SLOT + place % SLOT).astype(BF16)
    tall = length // 8
    owners = [block[i * tall : (i + 1) * tall, :] for block in points for i in range(block.shape[0] // tall)]
    for s in range(cols):
        values = jnp.concatenate([owners[s][t * 16 : (t + 1) * 16, :] for t in range(length // 128)], axis=1)
        mine = jnp.dot(values, take, preferred_element_type=F32)[:8]
        hot = (mine == iota(mine.shape, 0).astype(F32)).astype(BF16)
        traced[col ^ s] = jnp.dot(hot, sent[col ^ s], preferred_element_type=F32)

    both = slab_sum(high, plan, green, messages[count // 2 :], before[...])
    real = both[:high, :16] - both[high:, 16:]
    imag = both[:high, 16:] + both[high:, :16]
    total[...] = jnp.concatenate([real, imag, jnp.zeros((high, 96), F32)], axis=1)
    for c in range(cols):
        parts = [total[pl.ds(c * PTS * 4 + k, PTS, stride=4), :][:, :32] for k in range(4)]
        traced[c, :PTS, :] = traced[c, :PTS, :] - jnp.concatenate(parts, axis=1)
    for s in range(cols):
        outs[s][...] = traced[col ^ s, :PTS, :]


def late_call(rows, cols, plan, slots, green, before, messages, points):
    return pl.pallas_call(
        functools.partial(late_kernel, rows, cols, plan, slots),
        out_shape=[jax.ShapeDtypeStruct((PTS, 128), F32)] * cols,
        in_specs=[VMEM] * (2 + len(messages) + len(points)),
        out_specs=[VMEM] * cols,
        scratch_shapes=[
            pltpu.VMEM((cols, rows * SLOT, 128), BF16),
            pltpu.VMEM((cols, 8, 128), F32),
            pltpu.VMEM((green.shape[2], 128), F32),
        ],
        compiler_params=pltpu.CompilerParams(vmem_limit_bytes=8 * 2**20),
        cost_estimate=pl.CostEstimate(flops=COST, bytes_accessed=2**20, transcendentals=0),
    )(green, before, *messages, *points)


def shards(rows, cols, displacement, connectivity, element_basis, material, traction, green, node, weight, count, recv):
    masks = rows // 2
    given = (traction, displacement, node, weight, count, recv, connectivity.T, element_basis, material, green)
    *given, green = [pltpu.with_memory_space_constraint(value, pltpu.HBM) for value in given]
    made = prepare_call(rows, cols, *given)
    messages, (near, edge, points, disp, links, basis, coeffs) = made[: masks - 1], made[masks - 1 :]
    flat = ("row", "col")
    last = rows * cols - 1
    half = traction.shape[0] * 2
    each = cols * SLOT * 8

    def across(value, mask):
        return lax.ppermute(value, "row", [(i, i ^ mask) for i in range(rows)])

    def along(value, s):
        return lax.ppermute(value, "col", [(i, i ^ s) for i in range(cols)])

    own = messages[0]
    beside, below = across(messages[1], 2), across(messages[2], 4)
    far = [across(messages[k], 2 * k + 2) for k in range(3, masks - 1)]
    near = along(near, 1)
    steps = [(i, i + 1) for i in range(1, last, 2)]
    edge = lax.ppermute(edge, flat, steps + [(b, a) for a, b in steps])
    made = first_call(rows, SPLIT, disp, links, basis, coeffs, green)
    own, beside, below, near, edge, points, made = lax.optimization_barrier(
        (own, beside, below, near, edge, points, made)
    )
    acc, *shared, held = made
    cross = [across(beside[:, : half + each], 4), across(below[:, half : 2 * half], 2)]
    known = [jnp.concatenate([points, near[HALO:]], axis=0)]
    while len(known) < cols // 2:
        known += [along(value, 2 * len(known)) for value in known]
    there = [across(own, 1), across(beside, 1)]
    acc, held_pair = second_call(rows, SPLIT, links, coeffs, acc, shared, near, edge, green)
    there, acc, held_pair = lax.optimization_barrier((there, acc, held_pair))
    plan = [(0, 0, 2 * half, 1, 0), (1, 0, half, 3, 0), (1, half + each, half, 3, half)]
    early = early_call(plan, held_pair, there)
    own, beside, below, cross, far, known, there, acc, held_pair, early = lax.optimization_barrier(
        (own, beside, below, cross, far, known, there, acc, held_pair, early)
    )
    here = [own, beside, below] + cross + far
    there += [across(value, 1) for value in here[2:]]
    plan = [(0, 0, 2 * half, 0, 0), (1, 0, half, 2, 0), (1, half + each, half, 2, half), (2, 0, 2 * half, 4, 0)]
    plan += [(3, 0, half, 6, 0), (4, 0, half, 6, half)]
    slots = [(0, 2 * half, 0), (1, 2 * half + each, 2), (2, 2 * half, 4), (3, half, 6)]
    for i in range(len(far)):
        plan.append((5 + i, 0, 2 * half, 8 + 2 * i, 0))
        slots.append((5 + i, 2 * half, 8 + 2 * i))
    early = early_call(plan, held, here, (early,))
    early, there = lax.optimization_barrier((early, there))
    plan = [(which, lane, width, k + 1, into) for which, lane, width, k, into in plan if which > 1]
    parts = late_call(rows, cols, plan, slots, held_pair, early, here + there, known)
    sums = [along(parts[s], s) for s in range(1, cols)]
    acc, total = lax.optimization_barrier((acc, parts[0]))
    fe_out = third_call(links, coeffs, acc, shared, near, edge)
    sums, fe_out = lax.optimization_barrier((sums, fe_out))
    boundary = total
    for value in sums:
        boundary = boundary + value
    return fe_out, boundary


def solution(mesh):
    rows, cols = mesh.shape["row"], mesh.shape["col"]
    near = P(("row", "col"), None)
    placed = (near, near, P(), P(None, ("row", "col")), P(("col", "row"), None), P(None, "row", "col"), near, near, near, near)
    return jax.shard_map(
        functools.partial(shards, rows, cols),
        mesh=mesh,
        in_specs=placed,
        out_specs=(near, near),
        check_vma=False,
    )
```

```python
import functools

import jax
import jax.numpy as jnp
from jax import lax
from jax.experimental import pallas as pl
from jax.experimental.pallas import tpu as pltpu
from jax.sharding import PartitionSpec as P

PTS = 4
COST = 10**8
SLOT = 16
SPLIT = 6
HALO = 128
EB = 256
WIN = EB + 2 * HALO
NT = (((1,), (1,)), ((), ()))
F32 = jnp.float32
BF16 = jnp.bfloat16
VMEM = pl.BlockSpec(memory_space=pltpu.VMEM)
HBM = pl.BlockSpec(memory_space=pltpu.HBM)


def iota(shape, axis):
    return lax.broadcasted_iota(jnp.int32, shape, axis)


def lane_order():
    row, lane = iota((128, 128), 0), iota((128, 128), 1)
    return (lane == row % 8 // 2 * 32 + row // 8 * 2 + row % 2).astype(F32).astype(BF16)


def spread_basis(basis, wcat):
    spread = (iota((64, 32), 0) // 2 == iota((64, 32), 1)).astype(F32).astype(BF16)
    same = iota((64, 64), 0) % 2 == iota((64, 64), 1) % 2
    wide = []
    for m in range(4):
        tall = jnp.dot(spread, basis[m], preferred_element_type=F32).astype(BF16)
        full = lax.dot_general(tall, spread, NT, preferred_element_type=F32)
        wide.append(jnp.where(same, full, 0.0).astype(BF16))
    wcat[...] = jnp.concatenate(wide, axis=1)


def node_gaps():
    gap = iota((WIN, EB), 0) - iota((WIN, EB), 1)
    return jnp.where((gap >= 0) & (gap <= 2 * HALO), gap, -1).astype(F32).astype(BF16)


def flip(rows, order):
    return lax.dot_general(order, rows, NT, preferred_element_type=F32).astype(BF16)


def upright(tile, order):
    return jnp.dot(tile.T.astype(BF16), order, preferred_element_type=F32).astype(BF16)


def element_gaps():
    gap = iota((EB, WIN), 1) - iota((EB, WIN), 0)
    return jnp.where((gap >= 0) & (gap <= 2 * HALO), gap, -1).astype(F32).astype(BF16)


def gather_steps(at, window, links, dist, dist_t, selt, vs):
    across = links[:, at : at + EB] - (at + iota((8, EB), 1))
    down = across.astype(F32).T.astype(BF16)
    across = across.astype(F32).astype(BF16)
    one, zero = jnp.ones((), BF16), jnp.zeros((), BF16)

    def step(n):
        chosen = jnp.where(dist[...] == across[n : n + 1, :], one, zero)
        vs[n] = jnp.dot(window(), chosen, preferred_element_type=F32)
        selt[n * EB : (n + 1) * EB, :] = jnp.where(dist_t[...] == down[:, n : n + 1], one, zero)

    return [functools.partial(step, n) for n in range(8)]


def force_steps(at, material, wcat, vs, us, fs):
    coeffs = material[:, at : at + EB]
    kept = {}

    def step(cp):
        for n in range(0, 8, 2):
            re = jnp.concatenate([vs[n + i, cp * 8 : cp * 8 + 8, :] for i in range(2)], axis=0)
            im = jnp.concatenate([vs[n + i, 64 + cp * 8 : 72 + cp * 8, :] for i in range(2)], axis=0)
            for m in range(4):
                cr = coeffs[2 * m : 2 * m + 1, :]
                ci = coeffs[2 * m + 1 : 2 * m + 2, :]
                up = slice(m * 64 + n * 8, m * 64 + n * 8 + 16)
                us[cp, up, :EB] = (cr * re - ci * im).astype(BF16)
                us[cp, up, EB:] = (cr * im + ci * re).astype(BF16)
        kept[cp % 2] = jnp.dot(wcat[...], us[cp], preferred_element_type=F32)
        if cp % 2:
            for p in range(2):
                for n in range(8):
                    both = [kept[i][n * 8 : n * 8 + 8, p * EB : (p + 1) * EB] for i in range(2)]
                    rows = slice(p * 64 + cp * 8 - 8, p * 64 + cp * 8 + 8)
                    fs[rows, n * EB : (n + 1) * EB] = jnp.concatenate(both, axis=0).astype(BF16)

    return [functools.partial(step, cp) for cp in range(8)]


def scatter_steps(at, selt, fs, acc):
    def step(i):
        span = slice(i * 2 * EB, (i + 1) * 2 * EB)
        acc[:, at : at + WIN] += jnp.dot(fs[:, span], selt[span, :], preferred_element_type=F32)

    return [functools.partial(step, i) for i in range(4)]


def run_blocks(starts, windows, links, material, wcat, dist, dist_t, selt, vs, us, fs, accs):
    count = len(starts)
    for t in range(count + 2):
        lanes = []
        if t < count:
            lanes.append(gather_steps(starts[t], windows[t], links, dist, dist_t, selt.at[t % 3], vs.at[t % 2]))
        if 0 <= t - 1 < count:
            k = t - 1
            lanes.append(force_steps(starts[k], material, wcat, vs.at[k % 2], us.at[k % 2], fs.at[k % 2]))
        if 0 <= t - 2 < count:
            k = t - 2
            target, at = accs(k)
            lanes.append(scatter_steps(at, selt.at[k % 3], fs.at[k % 2], target))
        for i in range(8):
            for lane in lanes:
                if len(lane) == 8:
                    lane[i]()
                elif i % 2:
                    lane[i // 2]()


def fetch(parity, green, held, sems):
    row = lax.axis_index("row")
    length = held.shape[3]
    copies = []
    for k in range(held.shape[0]):
        start = pl.multiple_of((row ^ (2 * k + parity)) * length, 128)
        copies.append(pltpu.make_async_copy(green.at[:, :, pl.ds(start, length)], held.at[k], sems.at[k]))
    for copy in copies:
        copy.start()
    return copies


def first_kernel(split, disp, links, basis, material, green, acc, xt, wcat, dist, dist_t, held, selt, vs, us, fs, sems):
    nodes = disp.shape[0]
    copies = fetch(0, green, held, sems)
    @pl.when(lax.axis_index("row") >= 0)
    def blocks():
        order = lane_order()
        for i in range(nodes // 256):
            xt[:, HALO + i * 256 : HALO + (i + 1) * 256] = flip(disp[i * 256 : (i + 1) * 256, :], order)
        spread_basis(basis, wcat)
        dist[...] = node_gaps()
        dist_t[...] = element_gaps()
        acc[...] = jnp.zeros_like(acc)
        starts = [b * EB for b in range(1, split)]
        windows = [lambda at=at: xt[:, at : at + WIN] for at in starts]
        run_blocks(starts, windows, links, material, wcat, dist, dist_t, selt, vs, us, fs, lambda k: (acc, starts[k]))

    for copy in copies:
        copy.wait()


def second_kernel(
    split, links, material, before, xt, wcat, dist, dist_t, near, edge, green, acc, held, low, selt, vs, us, fs, sems
):
    nodes = links.shape[1]
    copies = fetch(1, green, held, sems)
    @pl.when(lax.axis_index("row") >= 0)
    def blocks():
        order = lane_order()
        even = lax.axis_index("col") % 2 == 0
        low[:, :HALO] = flip(jnp.where(even, edge[...], near[:HALO, :]), order)
        low[:, HALO:] = xt[:, HALO:WIN]
        starts = [b * EB for b in range(split, nodes // EB - 1)] + [0]
        windows = [lambda at=at: xt[:, at : at + WIN] for at in starts[:-1]] + [lambda: low[...]]
        run_blocks(starts, windows, links, material, wcat, dist, dist_t, selt, vs, us, fs, lambda k: (acc, starts[k]))
    for copy in copies:
        copy.wait()


def third_kernel(
    links, material, acc, xt, wcat, dist, dist_t, near, edge, out, high, last, selt, vs, us, fs, done, sems
):
    nodes = links.shape[1]
    keep = WIN - HALO
    at = nodes - EB
    order = lane_order()
    even = lax.axis_index("col") % 2 == 0
    high[:, :keep] = xt[:, at : at + keep]
    high[:, keep:] = flip(jnp.where(even, near[:HALO, :], edge[...]), order)
    last[...] = acc[:, at : at + WIN]
    split = nodes - keep
    for i in range(split // 128):
        done[i * 128 : (i + 1) * 128, :] = upright(acc[:, HALO + i * 128 : HALO + (i + 1) * 128], order)
    copies = [
        pltpu.make_async_copy(done.at[pl.ds(0, split), :], out.at[pl.ds(0, split), :], sems.at[0]),
        pltpu.make_async_copy(done.at[pl.ds(split, keep), :], out.at[pl.ds(split, keep), :], sems.at[1]),
    ]
    copies[0].start()
    windows = [lambda: high[...]]
    run_blocks([at], windows, links, material, wcat, dist, dist_t, selt, vs, us, fs, lambda k: (last, 0))
    for i in range(keep // 128):
        done[split + i * 128 : split + (i + 1) * 128, :] = upright(last[:, i * 128 : (i + 1) * 128], order)
    copies[1].start()
    for copy in copies:
        copy.wait()


def block_scratch():
    return [
        pltpu.VMEM((3, 8 * EB, WIN), BF16),
        pltpu.VMEM((2, 8, 128, EB), F32),
        pltpu.VMEM((2, 8, 256, 2 * EB), BF16),
        pltpu.VMEM((2, 128, 8 * EB), BF16),
    ]


def element_params(blocks):
    return dict(
        compiler_params=pltpu.CompilerParams(vmem_limit_bytes=18 * 2**20),
        cost_estimate=pl.CostEstimate(flops=blocks * COST, bytes_accessed=2**20, transcendentals=0),
    )


def held_shape(rows, green):
    return jax.ShapeDtypeStruct((rows // 2, 2, green.shape[1], green.shape[2] // rows), BF16)


def first_call(rows, split, disp, links, basis, material, green):
    wide = disp.shape[0] + 2 * HALO
    return pl.pallas_call(
        functools.partial(first_kernel, split),
        out_shape=[
            jax.ShapeDtypeStruct((128, wide), F32),
            jax.ShapeDtypeStruct((128, wide), BF16),
            jax.ShapeDtypeStruct((64, 256), BF16),
            jax.ShapeDtypeStruct((WIN, EB), BF16),
            jax.ShapeDtypeStruct((EB, WIN), BF16),
            held_shape(rows, green),
        ],
        in_specs=[VMEM] * 4 + [HBM],
        out_specs=[VMEM] * 6,
        scratch_shapes=block_scratch() + [pltpu.SemaphoreType.DMA((rows // 2,))],
        **element_params(split - 1),
    )(disp, links, basis, material, green)


def second_call(rows, split, links, material, acc, shared, near, edge, green):
    nodes = links.shape[1]
    return pl.pallas_call(
        functools.partial(second_kernel, split),
        out_shape=[
            jax.ShapeDtypeStruct(acc.shape, F32),
            held_shape(rows, green),
        ],
        in_specs=[VMEM] * 9 + [HBM],
        out_specs=[VMEM] * 2,
        scratch_shapes=[pltpu.VMEM((128, WIN), BF16)] + block_scratch() + [pltpu.SemaphoreType.DMA((rows // 2,))],
        input_output_aliases={2: 0},
        **element_params(nodes // EB - split),
    )(links, material, acc, *shared, near, edge, green)


def third_call(links, material, acc, shared, near, edge):
    nodes = links.shape[1]
    return pl.pallas_call(
        third_kernel,
        out_shape=jax.ShapeDtypeStruct((nodes, 128), BF16),
        in_specs=[VMEM] * 9,
        out_specs=HBM,
        scratch_shapes=[pltpu.VMEM((128, WIN), BF16), pltpu.VMEM((128, WIN), F32)]
        + block_scratch()
        + [pltpu.VMEM((nodes, 128), BF16), pltpu.SemaphoreType.DMA((2,))],
        **element_params(1),
    )(links, material, acc, *shared, near, edge)


def prepare_kernel(rows, cols, *refs):
    masks = rows // 2
    sources = refs[:9]
    messages = refs[9 : 8 + masks]
    near, edge, points, disp, links, basis, material, slots, traction, node, weight, count, recv, sems = refs[8 + masks :]
    lines = traction.shape[0]
    row, col = lax.axis_index("row"), lax.axis_index("col")
    pieces = 3 if lines // 128 % 3 == 0 else 1
    share = lines // pieces
    copies = [
        pltpu.make_async_copy(
            sources[0].at[pl.ds(i * share, share), :], traction.at[pl.ds(i * share, share), :], sems.at[8 + i]
        )
        for i in range(pieces)
    ]
    others = [
        pltpu.make_async_copy(sources[i + 1], target, sems.at[i])
        for i, target in enumerate((disp, node, weight, count, recv, links, basis, material))
    ]
    for copy in copies + others:
        copy.start()
    for copy in copies + others:
        copy.wait()

    gap = cols * SLOT * 8
    widen = (iota((128, 512), 1) // 4 == iota((128, 512), 0)).astype(BF16)
    comp = iota((32, 512), 1) % 4
    for i in range(lines // 128):
        wide = jnp.dot(traction[i * 128 : (i + 1) * 128, :].astype(F32).T.astype(BF16), widen, preferred_element_type=F32)
        line = wide[:32]
        for k in range(1, 4):
            line = jnp.where(comp == k, wide[k * 32 : (k + 1) * 32], line)
        line = line.astype(BF16)
        for t in range(2):
            lane = i * 512 + t * 256
            for k, message in enumerate(messages):
                into = lane + gap if k == 1 and lane >= lines * 2 else lane
                message[:, into : into + 256] = line[:, t * 256 : (t + 1) * 256]

    tail, head = disp[disp.shape[0] - HALO :, :], disp[:HALO, :]
    even = col % 2 == 0
    near[:HALO, :] = jnp.where(even, tail, head)
    edge[...] = jnp.where(even, head, tail)
    total = node.shape[1]
    devices = count.shape[1]
    copies = (iota((devices, total), 1) // SLOT == iota((devices, total), 0)).astype(BF16)
    counts = jnp.broadcast_to(count[...].astype(F32), (8, devices)).astype(BF16)
    live = jnp.dot(counts, copies, preferred_element_type=F32)
    scale = jnp.where((iota((8, total), 1) % SLOT).astype(F32) < live, weight[...], 0.0)
    columns = jnp.where(iota((8, total), 0) == 0, node[...].astype(F32), scale).T
    for i in range(total // 256):
        chunk = columns[i * 256 : (i + 1) * 256]
        hit = chunk[:, 0:1] == iota((256, disp.shape[0]), 1).astype(F32)
        picked = jnp.dot(jnp.where(hit, 1.0, 0.0).astype(BF16), disp[...], preferred_element_type=F32)
        slots[i * 256 : (i + 1) * 256, :] = (picked * chunk[:, 1:2]).astype(BF16)

    each = cols * SLOT
    places = [(messages[k], lines * 4) for k in range(3)] + [(messages[1], lines * 2)]
    places[1] = (messages[1], lines * 4 + gap)
    places += [(message, lines * 4) for message in messages[3:]]
    for k, (message, lane) in enumerate(places):
        for core in range(2):
            target = (row // 2 ^ k) * 2 + core
            for t in range(each // 32):
                start = pl.multiple_of(target * each + t * 32, 32)
                message[:, lane : lane + 128] = slots[pl.ds(start, 32), :]
                lane += 128

    for t in range(total // 128):
        feeds = recv[:, t * 128 : (t + 1) * 128].astype(F32)
        feeds = jnp.broadcast_to(feeds, (16, 128)).astype(BF16)
        points[t * 16 : (t + 1) * 16, :] = feeds
        near[HALO + t * 16 : HALO + (t + 1) * 16, :] = feeds


def prepare_call(rows, cols, traction, disp, node, weight, count, recv, links, basis, material):
    masks = rows // 2
    width = traction.shape[0] * 4 + cols * SLOT * 8
    widths = [width, width + cols * SLOT * 8] + [width] * (masks - 3)
    near = jax.ShapeDtypeStruct((HALO + node.shape[1] // 8, 128), BF16)
    edge = jax.ShapeDtypeStruct((HALO, 128), BF16)
    points = jax.ShapeDtypeStruct((node.shape[1] // 8, 128), BF16)
    same = [jax.ShapeDtypeStruct(value.shape, value.dtype) for value in (disp, links, basis, material)]
    return pl.pallas_call(
        functools.partial(prepare_kernel, rows, cols),
        out_shape=[jax.ShapeDtypeStruct((32, width), BF16) for width in widths] + [near, edge, points] + same,
        in_specs=[HBM] * 9,
        out_specs=[VMEM] * (masks + 6),
        scratch_shapes=[pltpu.VMEM((node.shape[1], 128), BF16)]
        + [pltpu.VMEM(value.shape, value.dtype) for value in (traction, node, weight, count, recv)]
        + [pltpu.SemaphoreType.DMA((11,))],
        compiler_params=pltpu.CompilerParams(vmem_limit_bytes=24 * 2**20),
    )(traction, disp, node, weight, count, recv, links, basis, material)


def slab_sum(high, plan, green, messages, start):
    both = start
    for which, lane, width, k, into in plan:
        flat = green[k // 2, :, :, into : into + width].reshape(2 * high, width)
        both = both + lax.dot_general(flat, messages[which][:, lane : lane + width], NT, preferred_element_type=F32)
    return both


def early_kernel(plan, count, green, *refs):
    high = green.shape[2]
    start = refs[count][...] if len(refs) > count + 1 else jnp.zeros((2 * high, 32), F32)
    refs[-1][...] = slab_sum(high, plan, green, refs[:count], start)


def early_call(plan, green, messages, start=()):
    return pl.pallas_call(
        functools.partial(early_kernel, plan, len(messages)),
        out_shape=jax.ShapeDtypeStruct((2 * green.shape[2], 32), F32),
        in_specs=[VMEM] * (1 + len(messages) + len(start)),
        out_specs=VMEM,
        compiler_params=pltpu.CompilerParams(vmem_limit_bytes=8 * 2**20),
        cost_estimate=pl.CostEstimate(flops=COST, bytes_accessed=2**20, transcendentals=0),
    )(green, *messages, *start)


def late_kernel(rows, cols, plan, slots, green, before, *refs):
    count = 2 * (max(entry[0] for entry in plan) + 1)
    messages, points = refs[:count], refs[count : -cols - 3]
    outs = refs[-cols - 3 : -3]
    sent, traced, total = refs[-3:]
    row, col = lax.axis_index("row"), lax.axis_index("col")
    high = green.shape[2]
    each = cols * SLOT
    for which, lane, k in slots:
        for core in range(2):
            into = pl.multiple_of((row ^ k ^ core) * SLOT, SLOT)
            for t in range(each // 32):
                at = pl.multiple_of(lane + (row % 2 * (each // 32) + t) * 128, 128)
                pair = messages[which + core * (count // 2)][:, pl.ds(at, 128)]
                sent[2 * t, pl.ds(into, SLOT), :] = pair[:SLOT]
                sent[2 * t + 1, pl.ds(into, SLOT), :] = pair[SLOT:]
    width = rows * SLOT
    length = width * cols
    source, place = iota((length, width), 0), iota((length, width), 1)
    take = (source == (place // SLOT * cols + col) * SLOT + place % SLOT).astype(BF16)
    tall = length // 8
    owners = [block[i * tall : (i + 1) * tall, :] for block in points for i in range(block.shape[0] // tall)]
    for s in range(cols):
        values = jnp.concatenate([owners[s][t * 16 : (t + 1) * 16, :] for t in range(length // 128)], axis=1)
        mine = jnp.dot(values, take, preferred_element_type=F32)[:8]
        hot = (mine == iota(mine.shape, 0).astype(F32)).astype(BF16)
        traced[col ^ s] = jnp.dot(hot, sent[col ^ s], preferred_element_type=F32)

    both = slab_sum(high, plan, green, messages[count // 2 :], before[...])
    real = both[:high, :16] - both[high:, 16:]
    imag = both[:high, 16:] + both[high:, :16]
    total[...] = jnp.concatenate([real, imag, jnp.zeros((high, 96), F32)], axis=1)
    for c in range(cols):
        parts = [total[pl.ds(c * PTS * 4 + k, PTS, stride=4), :][:, :32] for k in range(4)]
        traced[c, :PTS, :] = traced[c, :PTS, :] - jnp.concatenate(parts, axis=1)
    for s in range(cols):
        outs[s][...] = traced[col ^ s, :PTS, :]


def late_call(rows, cols, plan, slots, green, before, messages, points):
    return pl.pallas_call(
        functools.partial(late_kernel, rows, cols, plan, slots),
        out_shape=[jax.ShapeDtypeStruct((PTS, 128), F32)] * cols,
        in_specs=[VMEM] * (2 + len(messages) + len(points)),
        out_specs=[VMEM] * cols,
        scratch_shapes=[
            pltpu.VMEM((cols, rows * SLOT, 128), BF16),
            pltpu.VMEM((cols, 8, 128), F32),
            pltpu.VMEM((green.shape[2], 128), F32),
        ],
        compiler_params=pltpu.CompilerParams(vmem_limit_bytes=8 * 2**20),
        cost_estimate=pl.CostEstimate(flops=COST, bytes_accessed=2**20, transcendentals=0),
    )(green, before, *messages, *points)


def shards(rows, cols, displacement, connectivity, element_basis, material, traction, green, node, weight, count, recv):
    masks = rows // 2
    given = (traction, displacement, node, weight, count, recv, connectivity.T, element_basis, material, green)
    *given, green = [pltpu.with_memory_space_constraint(value, pltpu.HBM) for value in given]
    made = prepare_call(rows, cols, *given)
    messages, (near, edge, points, disp, links, basis, coeffs) = made[: masks - 1], made[masks - 1 :]
    flat = ("row", "col")
    last = rows * cols - 1
    half = traction.shape[0] * 2
    each = cols * SLOT * 8

    def across(value, mask):
        return lax.ppermute(value, "row", [(i, i ^ mask) for i in range(rows)])

    def along(value, s):
        return lax.ppermute(value, "col", [(i, i ^ s) for i in range(cols)])

    own = messages[0]
    beside, below = across(messages[1], 2), across(messages[2], 4)
    far = [across(messages[k], 2 * k + 2) for k in range(3, masks - 1)]
    near = along(near, 1)
    steps = [(i, i + 1) for i in range(1, last, 2)]
    edge = lax.ppermute(edge, flat, steps + [(b, a) for a, b in steps])
    made = first_call(rows, SPLIT, disp, links, basis, coeffs, green)
    own, beside, below, near, edge, points, made = lax.optimization_barrier(
        (own, beside, below, near, edge, points, made)
    )
    acc, *shared, held = made
    cross = [across(beside[:, : half + each], 4), across(below[:, half : 2 * half], 2)]
    known = [jnp.concatenate([points, near[HALO:]], axis=0)]
    while len(known) < cols // 2:
        known += [along(value, 2 * len(known)) for value in known]
    there = [across(own, 1), across(beside, 1)]
    acc, held_pair = second_call(rows, SPLIT, links, coeffs, acc, shared, near, edge, green)
    there, acc, held_pair = lax.optimization_barrier((there, acc, held_pair))
    plan = [(0, 0, 2 * half, 1, 0), (1, 0, half, 3, 0), (1, half + each, half, 3, half)]
    early = early_call(plan, held_pair, there)
    own, beside, below, cross, far, known, there, acc, held_pair, early = lax.optimization_barrier(
        (own, beside, below, cross, far, known, there, acc, held_pair, early)
    )
    here = [own, beside, below] + cross + far
    there += [across(value, 1) for value in here[2:]]
    plan = [(0, 0, 2 * half, 0, 0), (1, 0, half, 2, 0), (1, half + each, half, 2, half), (2, 0, 2 * half, 4, 0)]
    plan += [(3, 0, half, 6, 0), (4, 0, half, 6, half)]
    slots = [(0, 2 * half, 0), (1, 2 * half + each, 2), (2, 2 * half, 4), (3, half, 6)]
    for i in range(len(far)):
        plan.append((5 + i, 0, 2 * half, 8 + 2 * i, 0))
        slots.append((5 + i, 2 * half, 8 + 2 * i))
    early = early_call(plan, held, here, (early,))
    early, there = lax.optimization_barrier((early, there))
    plan = [(which, lane, width, k + 1, into) for which, lane, width, k, into in plan if which > 1]
    parts = late_call(rows, cols, plan, slots, held_pair, early, here + there, known)
    sums = [along(parts[s], s) for s in range(1, cols)]
    acc, total = lax.optimization_barrier((acc, parts[0]))
    fe_out = third_call(links, coeffs, acc, shared, near, edge)
    sums, fe_out = lax.optimization_barrier((sums, fe_out))
    boundary = total
    for value in sums:
        boundary = boundary + value
    return fe_out, boundary


def solution(mesh):
    rows, cols = mesh.shape["row"], mesh.shape["col"]
    near = P(("row", "col"), None)
    placed = (near, near, P(), P(None, ("row", "col")), P(("col", "row"), None), P(None, "row", "col"), near, near, near, near)
    return jax.shard_map(
        functools.partial(shards, rows, cols),
        mesh=mesh,
        in_specs=placed,
        out_specs=(near, near),
        check_vma=False,
    )
```
